256 devices in a mesh: dp: 4 (over y), expert: 64 (over x, z, core).
Axes of the slice: x: 4, y: 4, z: 8, core: 2. Of those that a mesh axis runs over, the one named last changes fastest.
Arguments:
- activations: bfloat16 [32768, 4096], P(('dp', 'expert')), may hold values from -24 to 24
- cotangent: bfloat16 [32768, 4096], P(('dp', 'expert')), may hold values from -24 to 24
- basis: bfloat16 [4096, 512], replicated, may hold values from -0.09375 to 0.09375
- route_ids: int32 [32768, 8], P(('dp', 'expert')), may hold values from 0 to 127, all different within a row; in each aligned block of 128 rows (0 to 127, 128 to 255, ...) at most 12 rows name the same one
- route_weights: float32 [32768, 8], P(('dp', 'expert')), may hold values from 0.05 to 0.5
- proj_in: bfloat16 [128, 512, 128], P('expert'), may hold values from -0.25 to 0.25
- gate_factor: bfloat16 [128, 128, 1536], P('expert'), may hold values from -0.5 to 0.5
- up_factor: bfloat16 [128, 128, 1536], P('expert'), may hold values from -0.5 to 0.5
- down_factor: bfloat16 [128, 1536, 128], P('expert'), may hold values from -0.15625 to 0.15625
- proj_out: bfloat16 [128, 128, 512], P('expert'), may hold values from -0.5 to 0.5
Outputs:
- grad_input: bfloat16 [32768, 4096], P(('dp', 'expert'))
- grad_route: float32 [32768, 8], P(('dp', 'expert'))
- grad_basis: float32 [4096, 512], P(('dp', 'expert'))
- grad_proj_in: float32 [128, 512, 128], P('expert', 'dp')
- grad_gate: float32 [128, 128, 1536], P('expert', None, 'dp')
- grad_up: float32 [128, 128, 1536], P('expert', None, 'dp')
- grad_down: float32 [128, 1536, 128], P('expert', 'dp')
- grad_proj_out: float32 [128, 128, 512], P('expert', None, 'dp')
The draws below stay inside these ranges and needn't reach their ends.
Inputs may be any that keep to these rules, and one draw needn't show every extreme that they name: `route_ids`: among the 128 rows of one device no expert is named by more than 12 of them, a bound that some block reaches; each row names 8 different experts.
All inputs are finite; a program needn't handle non-finite values.
Results may differ from the reference program's by a relative error of at most 0.025.
Values may be sent and summed in bfloat16 or wider, within the bound.
No kernel may reach another device: no remote copies, remote signals or barrier semaphores. Data moves between devices by JAX's collectives and lax.ppermute only.
A program may use at most 128 MiB of HBM per device.

```python
import math
import jax
import jax.numpy as jnp
import numpy as np
from jax import lax

D = 4096
FF = 1536
R = 512
K = 128
TOP = 8
TOK_DEV = 128
EXPERTS = 128
TOKENS = 32768
CAP = 12


def strengthened(array, own_key, source, target, blocks, factor):
    def block_of(axis_at):
        return (jnp.arange(array.shape[axis_at]) // (array.shape[axis_at] // blocks)).reshape((-1,) + (1,) * (array.ndim - 1 - axis_at))

    one_side = jax.random.permutation(own_key, blocks)[block_of(target)]
    other_side = (block_of(target) + blocks // 2) % blocks
    return jnp.where((block_of(source) == one_side) | (block_of(source) == other_side), factor * array, array)


def levels(rng, shape, pieces, least, largest):
    def one(axis_at, shards_of):
        heights = jax.random.uniform(jax.random.fold_in(jax.random.fold_in(rng, 6), axis_at), (shards_of,), jnp.float32, least / len(pieces), largest / len(pieces))
        return jnp.repeat(jnp.exp(heights), shape[axis_at] // shards_of).reshape((-1,) + (1,) * (len(shape) - axis_at - 1))

    level = one(*pieces[0])
    for cut in pieces[1:]:
        level = level * one(*cut)
    return level


def routed_block(stream_key, own, number, rows, number_of, top, most, skew):
    order = jax.random.permutation(stream_key, number_of)
    packed, ordinary = portions_of(number_of, rows * top, most, skew, True), portions_of(number_of, rows * top, most, skew, False)
    places = jnp.arange(number_of)

    def named(lengths, offset_by):
        used = int((lengths > 0).sum())
        fixed = max(1, used // 4)
        moved = fixed + (places - fixed + offset_by * (used - fixed)) % max(1, number_of - fixed)
        return jnp.zeros((number_of,), jnp.int32).at[order[jnp.where(places < fixed, places, moved)]].set(jnp.asarray(lengths, jnp.int32))

    lengths = jnp.where(number % 4 == 0, named(packed, number // 4), named(ordinary, number - number // 4 - 1))
    mixed = jax.random.permutation(jax.random.fold_in(own, 3), number_of)
    donor, receiver = mixed[0:number_of // 2 * 2:2], mixed[1:number_of // 2 * 2:2]
    margin = jnp.minimum(lengths[donor] - 1, most - lengths[receiver]) // 2
    margin = jnp.where((donor == order[0]) | (receiver == order[0]) | (lengths[receiver] == 0), 0, jnp.maximum(margin, 0))
    moved = jax.random.randint(jax.random.fold_in(own, 4), (number_of // 2,), 0, 1 << 20) % (margin + 1)
    lengths = lengths.at[donor].add(-moved).at[receiver].add(moved)
    labels = jnp.searchsorted(jnp.cumsum(lengths), jnp.arange(rows * top), side="right").astype(jnp.int32)
    listing = labels.reshape(top, rows).T
    listing = listing[jax.random.permutation(jax.random.fold_in(own, 1), rows)]
    offset_by = jax.random.randint(jax.random.fold_in(own, 2), (rows, 1), 0, top)
    return jnp.take_along_axis(listing, (jnp.arange(top)[None, :] + offset_by) % top, axis=1)


def portions_of(count, total, reach, skew, full):
    portions = [(1 << 20) // math.isqrt(grade ** skew) + 1 for grade in range(1, count + 1)]
    largest = reach if full else min(reach, max(-(-total // count), total * portions[0] // sum(portions)))
    least = 1 if total - largest >= count - 1 else 0
    given, surplus = [largest] + [least] * (count - 1), total - largest - least * (count - 1)
    while surplus > 0:
        movable = [i for i in range(1, count) if given[i] < largest] or [i for i in range(1, count) if given[i] < reach]
        pool, remaining = sum([portions[i] for i in movable]), surplus
        for i in movable:
            more = min(reach - given[i], max(1, remaining * portions[i] // pool), surplus)
            given[i] = given[i] + more
            surplus = surplus - more
    return np.array(given)


def scatter_about(stream_key, dims, spread, limit, shards=(), kind=jnp.bfloat16):
    gain = levels(stream_key, dims, shards, -0.22, 0.18) if shards else 1.0
    result = jax.random.normal(stream_key, dims, jnp.float32) * spread * gain
    return jnp.minimum(jnp.maximum(result, -limit), limit).astype(kind)


def bell_draw_with(rng, dims, deviation, reach, pieces, heavy, held_as=jnp.bfloat16):
    drawn = deviation * jax.random.normal(rng, dims, jnp.float32)
    if pieces:
        drawn = drawn * levels(rng, dims, pieces, -0.22, 0.18)
    return jnp.clip(strengthened(drawn, jax.random.fold_in(rng, 3), *heavy), -reach, reach).astype(held_as)


def setup_inputs(seed: int = 0) -> dict:
    seeds = jax.random.split(jax.random.key(seed), 11)
    activations = bell_draw_with(seeds[0], (TOKENS, D), 1.0, 24.0, ((0, 256),), (0, 1, 256, 6.0))
    cotangent = bell_draw_with(seeds[1], (TOKENS, D), 1.0, 24.0, ((0, 256),), (0, 1, 256, 6.0))
    basis = scatter_about(seeds[2], (D, R), D ** -0.5, 0.09375)
    route_ids_keys = jax.random.split(jax.random.fold_in(seeds[3], 1), TOKENS // TOK_DEV)
    route_ids_turns = jax.random.permutation(jax.random.fold_in(seeds[3], 3), TOKENS // TOK_DEV)
    route_ids = jax.vmap(lambda own, number: routed_block(jax.random.fold_in(seeds[3], 2), own, number, TOK_DEV, EXPERTS, TOP, CAP, 2))(route_ids_keys, route_ids_turns).reshape((TOKENS, TOP))
    route_weights = jnp.clip(jnp.exp(math.log(0.5) - 2.3025851 * jax.random.uniform(seeds[4], (TOKENS, TOP), jnp.float32) ** levels(seeds[4], (TOKENS, TOP), ((0, 256),), -0.2, 0.2)), 0.05, 0.5)
    proj_in = scatter_about(seeds[5], (EXPERTS, R, K), R ** -0.5, 0.25, ((0, 64),))
    gate_factor = scatter_about(seeds[6], (EXPERTS, K, FF), K ** -0.5, 0.5, ((0, 64),))
    up_factor = scatter_about(seeds[7], (EXPERTS, K, FF), K ** -0.5, 0.5, ((0, 64),))
    down_factor = scatter_about(seeds[8], (EXPERTS, FF, K), FF ** -0.5, 0.15625, ((0, 64),))
    proj_out = scatter_about(seeds[9], (EXPERTS, K, R), K ** -0.5, 0.5, ((0, 64),))
    return dict(activations=activations, cotangent=cotangent, basis=basis, route_ids=route_ids, route_weights=route_weights, proj_in=proj_in, gate_factor=gate_factor, up_factor=up_factor, down_factor=down_factor, proj_out=proj_out)


def silu_parts(pre):
    sig = jax.nn.sigmoid(pre)
    return pre * sig, sig * (1.0 + pre * (1.0 - sig))


def expert_rows(coords, scaled, proj_in, gate_factor, up_factor, down_factor, proj_out):
    f32 = jnp.float32
    codes = jnp.dot(coords, proj_in, preferred_element_type=f32).astype(jnp.bfloat16)
    gate_pre = jnp.dot(codes, gate_factor, preferred_element_type=f32)
    up_pre = jnp.dot(codes, up_factor, preferred_element_type=f32)
    active, slope = silu_parts(gate_pre)
    hidden = (active * up_pre).astype(jnp.bfloat16)
    narrow = jnp.dot(hidden, down_factor, preferred_element_type=f32).astype(jnp.bfloat16)
    outcome = jnp.dot(narrow, proj_out, preferred_element_type=f32).astype(jnp.bfloat16)
    g_out = jnp.dot(narrow.T, scaled, preferred_element_type=f32)
    d_narrow = jnp.dot(scaled, proj_out.T, preferred_element_type=f32).astype(jnp.bfloat16)
    g_down = jnp.dot(hidden.T, d_narrow, preferred_element_type=f32)
    d_hidden = jnp.dot(d_narrow, down_factor.T, preferred_element_type=f32)
    d_gate = (d_hidden * up_pre * slope).astype(jnp.bfloat16)
    d_up = (d_hidden * active).astype(jnp.bfloat16)
    g_gate = jnp.dot(codes.T, d_gate, preferred_element_type=f32)
    g_up = jnp.dot(codes.T, d_up, preferred_element_type=f32)
    d_codes = (jnp.dot(d_gate, gate_factor.T, preferred_element_type=f32)
               + jnp.dot(d_up, up_factor.T, preferred_element_type=f32)).astype(jnp.bfloat16)
    g_in = jnp.dot(coords.T, d_codes, preferred_element_type=f32)
    d_coords = jnp.dot(d_codes, proj_in.T, preferred_element_type=f32).astype(jnp.bfloat16)
    return outcome, d_coords, (g_in, g_gate, g_up, g_down, g_out)


def reference(activations, cotangent, basis, route_ids, route_weights, proj_in, gate_factor, up_factor, down_factor, proj_out):
    f32 = jnp.float32
    coords = jnp.dot(activations, basis, preferred_element_type=f32).astype(jnp.bfloat16)
    back = jnp.dot(cotangent, basis, preferred_element_type=f32).astype(jnp.bfloat16)
    sources = TOKENS // TOK_DEV
    blocks = route_ids.reshape(sources, TOK_DEV * TOP).astype(jnp.int32)

    def slots_of(block):
        onehot = (block[:, None] == jnp.arange(EXPERTS, dtype=jnp.int32)[None, :]).astype(jnp.int32)
        return (jnp.sum(jnp.cumsum(onehot, axis=0) * onehot, axis=1) - 1).astype(jnp.int32)

    slots = lax.map(slots_of, blocks)
    anchor = jnp.arange(sources, dtype=jnp.int32)[:, None]
    place = (blocks * (sources * CAP) + anchor * CAP + slots).reshape(-1).astype(jnp.int32)
    total = TOKENS * TOP
    table = jnp.full((EXPERTS * sources * CAP,), total, jnp.int32)
    table = table.at[place].set(jnp.arange(total, dtype=jnp.int32)).reshape(EXPERTS, sources * CAP)
    coords_pad = jnp.concatenate([coords, jnp.zeros((1, R), jnp.bfloat16)], axis=0)
    back_pad = jnp.concatenate([back, jnp.zeros((1, R), jnp.bfloat16)], axis=0)
    weight_pad = jnp.concatenate([route_weights.reshape(-1).astype(f32), jnp.zeros((1,), f32)], axis=0)

    def step(carry, inputs):
        grad_coords, mixed, grad_route = carry
        entry, p_in, g_fac, u_fac, d_fac, p_out = inputs
        token = (entry // TOP).astype(jnp.int32)
        rows = coords_pad[token]
        weight = weight_pad[entry]
        back_rows = back_pad[token].astype(f32)
        scaled = (weight[:, None] * back_rows).astype(jnp.bfloat16)
        outcome, d_coords, grads = expert_rows(rows, scaled, p_in, g_fac, u_fac, d_fac, p_out)
        outcome32 = outcome.astype(f32)
        grad_coords = grad_coords.at[token].add(d_coords.astype(f32), mode="drop")
        mixed = mixed.at[token].add(weight[:, None] * outcome32, mode="drop")
        grad_route = grad_route.at[entry].add(jnp.sum(back_rows * outcome32, axis=1), mode="drop")
        return (grad_coords, mixed, grad_route), grads

    start = (jnp.zeros((TOKENS, R), f32), jnp.zeros((TOKENS, R), f32), jnp.zeros((total,), f32))
    (grad_coords, mixed, grad_route), grads = lax.scan(
        step, start, (table, proj_in, gate_factor, up_factor, down_factor, proj_out))
    dz = grad_coords.astype(jnp.bfloat16)
    mixed_b = mixed.astype(jnp.bfloat16)
    grad_input = jnp.dot(dz, basis.T, preferred_element_type=f32).astype(jnp.bfloat16)
    grad_basis = (jnp.dot(activations.T, dz, preferred_element_type=f32)
                  + jnp.dot(cotangent.T, mixed_b, preferred_element_type=f32))
    return (grad_input, grad_route.reshape(TOKENS, TOP), grad_basis,
            grads[0], grads[1], grads[2], grads[3], grads[4])
```

```python
import jax
import jax.numpy as jnp
from jax import lax
from jax.sharding import Mesh
from jax.sharding import PartitionSpec as P

TOP = 8
EXP_DEV = 2
TOK_DEV = 128
EXPERT = ("x", "z", "c")
ALL = ("dp", "x", "z", "c")


def silu_parts(pre):
    sig = jax.nn.sigmoid(pre)
    return (pre * sig, sig * (1.0 + pre * (1.0 - sig)))


def exchange_sum(parts, axis):
    got = lax.all_to_all(parts, axis, split_axis=0, concat_axis=0, tiled=True)
    return jnp.sum(got.astype(jnp.float32), axis=0)


def scatter_over_dp(grad, dim):
    n = lax.axis_size("dp")
    shape = grad.shape[:dim] + (n, grad.shape[dim] // n) + grad.shape[dim + 1 :]
    parts = jnp.moveaxis(grad.astype(jnp.bfloat16).reshape(shape), dim, 0)
    return exchange_sum(parts, "dp")


def scatter_over_all(part):
    bf16 = jnp.bfloat16
    y, x, z = lax.axis_size("dp"), lax.axis_size("x"), lax.axis_size("z")
    width = part.shape[1]
    rows = part.shape[0] // (y * x * z * 2)
    pair = part.astype(bf16).reshape(y * x * z, 2, rows, width)
    core = lax.axis_index("c")
    kept = lax.dynamic_index_in_dim(pair, core, 1, keepdims=False)
    sent = lax.dynamic_index_in_dim(pair, 1 - core, 1, keepdims=False)
    other = lax.ppermute(sent, "c", [(0, 1), (1, 0)])
    total = (kept.astype(jnp.float32) + other.astype(jnp.float32)).astype(bf16)
    total = exchange_sum(total.reshape(y, x, z, rows, width), "dp").astype(bf16)
    total = exchange_sum(total, "x").astype(bf16)
    return exchange_sum(total, "z")


def per_device(
    activations,
    cotangent,
    basis,
    route_ids,
    route_weights,
    proj_in,
    gate_factor,
    up_factor,
    down_factor,
    proj_out,
):
    f32 = jnp.float32
    bf16 = jnp.bfloat16
    n_expert = lax.axis_size(EXPERT)
    experts = EXP_DEV * n_expert
    capacity = max(2, 3 * TOK_DEV * TOP // (2 * experts))
    width = basis.shape[1]
    coords = jnp.dot(activations, basis, preferred_element_type=f32).astype(bf16)
    back = jnp.dot(cotangent, basis, preferred_element_type=f32).astype(bf16)
    flat_ids = route_ids.reshape(-1)
    onehot = (flat_ids[:, None] == jnp.arange(experts, dtype=jnp.int32)[None, :]).astype(jnp.int32)
    slots = jnp.sum(jnp.cumsum(onehot, axis=0) * onehot, axis=1) - 1
    place = flat_ids * capacity + slots
    weights = route_weights.reshape(-1)
    back_rep = jnp.repeat(back, TOP, axis=0)
    coord_rep = jnp.repeat(coords, TOP, axis=0)
    scaled_rep = (weights[:, None] * back_rep.astype(f32)).astype(bf16)
    send_coords = jnp.zeros((experts * capacity, width), bf16).at[place].set(coord_rep)
    send_scaled = jnp.zeros((experts * capacity, width), bf16).at[place].set(scaled_rep)
    send_coords = send_coords.reshape(n_expert, EXP_DEV * capacity, width)
    send_scaled = send_scaled.reshape(n_expert, EXP_DEV * capacity, width)
    got_coords, got_scaled = (
        lax.all_to_all(send_coords, EXPERT, split_axis=0, concat_axis=0, tiled=True),
        lax.all_to_all(send_scaled, EXPERT, split_axis=0, concat_axis=0, tiled=True),
    )
    rows = got_coords.reshape(n_expert, EXP_DEV, capacity, width)
    scaled = got_scaled.reshape(n_expert, EXP_DEV, capacity, width)
    codes = jnp.einsum("secr,erk->seck", rows, proj_in, preferred_element_type=f32).astype(bf16)
    gate_pre = jnp.einsum("seck,ekf->secf", codes, gate_factor, preferred_element_type=f32)
    up_pre = jnp.einsum("seck,ekf->secf", codes, up_factor, preferred_element_type=f32)
    active, slope = silu_parts(gate_pre)
    hidden = (active * up_pre).astype(bf16)
    narrow = jnp.einsum("secf,efk->seck", hidden, down_factor, preferred_element_type=f32).astype(
        bf16
    )
    outcome = jnp.einsum("seck,ekr->secr", narrow, proj_out, preferred_element_type=f32).astype(
        bf16
    )
    g_out = jnp.einsum("seck,secr->ekr", narrow, scaled, preferred_element_type=f32)
    d_narrow = jnp.einsum("secr,ekr->seck", scaled, proj_out, preferred_element_type=f32).astype(
        bf16
    )
    g_down = jnp.einsum("secf,seck->efk", hidden, d_narrow, preferred_element_type=f32)
    d_hidden = jnp.einsum("seck,efk->secf", d_narrow, down_factor, preferred_element_type=f32)
    d_gate = (d_hidden * up_pre * slope).astype(bf16)
    d_up = (d_hidden * active).astype(bf16)
    g_gate = jnp.einsum("seck,secf->ekf", codes, d_gate, preferred_element_type=f32)
    g_up = jnp.einsum("seck,secf->ekf", codes, d_up, preferred_element_type=f32)
    d_codes = (
        jnp.einsum("secf,ekf->seck", d_gate, gate_factor, preferred_element_type=f32)
        + jnp.einsum("secf,ekf->seck", d_up, up_factor, preferred_element_type=f32)
    ).astype(bf16)
    g_in = jnp.einsum("secr,seck->erk", rows, d_codes, preferred_element_type=f32)
    d_coords = jnp.einsum("seck,erk->secr", d_codes, proj_in, preferred_element_type=f32).astype(
        bf16
    )
    send_grad = d_coords.reshape(n_expert, EXP_DEV * capacity, width)
    send_out = outcome.reshape(n_expert, EXP_DEV * capacity, width)
    got_grad, got_out = (
        lax.all_to_all(send_grad, EXPERT, split_axis=0, concat_axis=0, tiled=True),
        lax.all_to_all(send_out, EXPERT, split_axis=0, concat_axis=0, tiled=True),
    )
    grad_rows = got_grad.reshape(experts * capacity, width)[place].astype(f32)
    out_rows = got_out.reshape(experts * capacity, width)[place].astype(f32)
    grad_route = jnp.sum(back_rep.astype(f32) * out_rows, axis=1).reshape(TOK_DEV, TOP)
    dz = jnp.sum(grad_rows.reshape(TOK_DEV, TOP, width), axis=1).astype(bf16)
    mixed = jnp.sum((weights[:, None] * out_rows).reshape(TOK_DEV, TOP, width), axis=1).astype(bf16)
    grad_input = lax.dot_general(
        dz, basis, (((1,), (1,)), ((), ())), preferred_element_type=f32
    ).astype(bf16)
    part = jnp.einsum("td,tr->dr", activations, dz, preferred_element_type=f32) + jnp.einsum(
        "td,tr->dr", cotangent, mixed, preferred_element_type=f32
    )
    grad_basis = scatter_over_all(part)
    grad_proj_in = scatter_over_dp(g_in, 1)
    grad_gate = scatter_over_dp(g_gate, 2)
    grad_up = scatter_over_dp(g_up, 2)
    grad_down = scatter_over_dp(g_down, 1)
    grad_proj_out = scatter_over_dp(g_out, 2)
    return (
        grad_input,
        grad_route,
        grad_basis,
        grad_proj_in,
        grad_gate,
        grad_up,
        grad_down,
        grad_proj_out,
    )


def solution(mesh):
    fine = Mesh(mesh.devices.reshape(mesh.shape["dp"], 4, -1, 2), ALL)
    in_specs = (
        P(ALL, None),
        P(ALL, None),
        P(),
        P(ALL, None),
        P(ALL, None),
        P(EXPERT, None, None),
        P(EXPERT, None, None),
        P(EXPERT, None, None),
        P(EXPERT, None, None),
        P(EXPERT, None, None),
    )
    out_specs = (
        P(ALL, None),
        P(ALL, None),
        P(ALL, None),
        P(EXPERT, "dp", None),
        P(EXPERT, None, "dp"),
        P(EXPERT, None, "dp"),
        P(EXPERT, "dp", None),
        P(EXPERT, None, "dp"),
    )
    return jax.shard_map(
        per_device, mesh=fine, in_specs=in_specs, out_specs=out_specs, check_vma=False
    )
```

```python
import functools

import jax
import jax.numpy as jnp
from jax import lax
from jax.experimental import pallas as pl
from jax.experimental.pallas import tpu as pltpu
from jax.sharding import Mesh
from jax.sharding import PartitionSpec as P

EXP_DEV = 2
CORES = 2
NX = 4
NZ = 8
NY = 4
INFO = 16
EXPERT = ("x", "z", "c")
ALL = ("dp", "x", "z", "c")
BLOCKS = (0, -1, -2, -3, 1, 2, 3, 4)
OWNERS = ((0, 0), (0, 1), (1, 0), (1, 1), (3, 0), (3, 1), (2, 0), (2, 1))
f32 = jnp.float32
bf16 = jnp.bfloat16
MIB = 1024 * 1024


def from_z(value, step):
    return lax.ppermute(value, "z", [((z + step) % NZ, z) for z in range(NZ)])


def from_x(value, step):
    return lax.ppermute(value, "x", [((x + step) % NX, x) for x in range(NX)])


def from_y(value, step):
    return lax.ppermute(value, "dp", [((y + step) % NY, y) for y in range(NY)])


def from_core(value):
    return lax.ppermute(value, "c", [(0, 1), (1, 0)])


def to_owner(value, owner, back=False):
    dx, dc = owner
    pairs = [(x * CORES + c, (x + dx) % NX * CORES + (c ^ dc)) for x in range(NX) for c in range(CORES)]
    if back:
        pairs = [(b, a) for a, b in pairs]
    return lax.ppermute(value, ("x", "c"), pairs)


def exchange_sum(parts, axis):
    got = lax.all_to_all(parts, axis, split_axis=0, concat_axis=0, tiled=True)
    return jnp.sum(got.astype(f32), axis=0)


def call(kernel, grid, in_specs, out_specs, out_shape, scratch, cost, prefetch=0):
    return pl.pallas_call(
        kernel,
        grid_spec=pltpu.PrefetchScalarGridSpec(
            num_scalar_prefetch=prefetch,
            grid=grid,
            in_specs=in_specs,
            out_specs=out_specs,
            scratch_shapes=scratch,
        ),
        out_shape=out_shape,
        cost_estimate=pl.CostEstimate(flops=cost[0], bytes_accessed=cost[1], transcendentals=0),
        compiler_params=pltpu.CompilerParams(
            vmem_limit_bytes=24 * MIB, dimension_semantics=("arbitrary",) * len(grid)
        ),
    )


def place_of(device):
    core, rest = lax.rem(device, CORES), lax.div(device, CORES)
    z, rest = lax.rem(rest, NZ), lax.div(rest, NZ)
    return lax.div(rest, NX), lax.rem(rest, NX), z, core


def expert_of(device, row):
    _, x, z, core = place_of(device)
    dx, dc = OWNERS[row // EXP_DEV]
    core = 1 - core if dc else core
    return ((lax.rem(x + dx, NX) * NZ + z) * CORES + core) * EXP_DEV + row % EXP_DEV


def whole(shape):
    return pl.BlockSpec(shape, lambda *_: (0,) * len(shape))


def one_hot(route_ref, row, slots, tokens):
    place = lax.broadcasted_iota(jnp.int32, (slots, tokens), 0).astype(f32)
    return place == route_ref[pl.ds(row, 1), :]


def embed_kernel(_, act_ref, cot_ref, basis_ref, ids_ref, w_ref, out_ref, parts_ref, acc):
    k = pl.program_id(0)
    tok = act_ref.shape[0]
    top = ids_ref.shape[0]

    @pl.when(k == 0)
    def _():
        acc[...] = jnp.zeros_like(acc)

    both = jnp.concatenate([act_ref[...], cot_ref[...]], axis=0)
    parts_ref[0] = both
    acc[...] += jnp.dot(both, basis_ref[...], preferred_element_type=f32)

    @pl.when(k == pl.num_programs(0) - 1)
    def _():
        out_ref[: 2 * tok] = acc[...].astype(bf16)
        ids = ids_ref[...].astype(f32)
        weights = w_ref[...]
        high = weights.astype(bf16).astype(f32)
        rest = jnp.zeros((top, acc.shape[1] - 3 * tok), f32)
        info = jnp.concatenate([ids, high, weights - high, rest], axis=1)
        info = jnp.concatenate([info, jnp.zeros((INFO - top, acc.shape[1]), f32)], axis=0)
        out_ref[2 * tok :] = info.astype(bf16)


def dispatch_kernel(cap, top, *refs):
    (device_ref, tri_ref), refs = refs[:2], refs[2:]
    blocks, refs = refs[: len(BLOCKS)], refs[len(BLOCKS) :]
    (mine_ref, other_ref), refs = refs[:2], refs[2:]
    owners = [ref.at[i] for i in range(NX) for ref in (mine_ref, other_ref)]
    out_ref, route_ref, coords_out, back_out, coords_ref, back_ref, sem = refs
    tok = tri_ref.shape[0]
    tokens = coords_ref.shape[0]
    slots = len(BLOCKS) * cap
    pair = owners[0].shape[0] // 2
    rank = pair // EXP_DEV
    rows = len(OWNERS) * EXP_DEV
    line = lax.broadcasted_iota(jnp.int32, (rows, 1), 0)
    names = jnp.zeros((rows, 1), f32)
    for row in range(rows):
        names = jnp.where(line == row, expert_of(device_ref[0], row).astype(f32), names)
    for s in range(len(BLOCKS)):
        at = slice(s * tok, (s + 1) * tok)
        coords_ref[at, :] = blocks[s][:tok]
        back_ref[at, :] = blocks[s][tok : 2 * tok]
        info = blocks[s][2 * tok :].astype(f32)
        ids = info[:top, :tok]
        weights = info[:top, tok : 2 * tok] + info[:top, 2 * tok : 3 * tok]
        member = jnp.zeros((rows, tok), f32)
        weighted = jnp.zeros((rows, tok), f32)
        for k in range(top):
            hit = names == ids[k : k + 1, :]
            member = jnp.where(hit, 1.0, member)
            weighted = jnp.where(hit, weights[k : k + 1, :], weighted)
        rank_in = jnp.dot(member.astype(bf16), tri_ref[...], preferred_element_type=f32)
        route_ref[:rows, at] = jnp.where(member > 0.0, rank_in - 1.0 + s * cap, -1.0)
        route_ref[rows : 2 * rows, at] = weighted
        route_ref[2 * rows :, at] = ids
    copies = [
        pltpu.make_async_copy(coords_ref, coords_out, sem.at[0]),
        pltpu.make_async_copy(back_ref, back_out, sem.at[1]),
    ]
    for copy in copies:
        copy.start()
    nt = (((1,), (1,)), ((), ()))
    for i, w_ref in enumerate(owners):
        codes = lax.dot_general(
            coords_ref[...], w_ref[:pair], nt, preferred_element_type=f32
        ).astype(bf16)
        cross = lax.dot_general(
            back_ref[...], w_ref[pair:], nt, preferred_element_type=f32
        ).astype(bf16)
        for j in range(EXP_DEV):
            row = i * EXP_DEV + j
            hit = one_hot(route_ref, row, slots, tokens)
            pick = jnp.where(hit, 1.0, 0.0).astype(bf16)
            weight = jnp.sum(
                jnp.where(hit, route_ref[rows + row : rows + row + 1, :], 0.0),
                axis=1,
                keepdims=True,
            )
            cols = slice(j * rank, (j + 1) * rank)
            both = jnp.concatenate([codes[:, cols], cross[:, cols]], axis=1)
            picked = jnp.dot(pick, both, preferred_element_type=f32)
            out_ref[i, j, :, 0:rank] = picked[:, :rank].astype(bf16)
            out_ref[i, j, :, rank:] = (weight * picked[:, rank:]).astype(bf16)
    for copy in copies:
        copy.wait()


def expert_kernel(_, *refs):
    given_refs, refs = refs[: len(OWNERS)], refs[len(OWNERS) :]
    (gate_ref, up_ref, down_ref), refs = refs[:3], refs[3:]
    outs, refs = refs[: len(OWNERS)], refs[len(OWNERS) :]
    grads_ref, narrow_acc, codes_acc, in_ref, out_ref, sem = refs
    e, f = pl.program_id(0), pl.program_id(1)
    slots = given_refs[0].shape[1]

    @pl.when(f == 0)
    def _():
        for i, ref in enumerate(given_refs):
            in_ref[i * slots : (i + 1) * slots] = ref[e]

    rank = gate_ref.shape[1]
    given = in_ref[...]
    codes, d_narrow = given[:, :rank], given[:, rank:]
    gate, up, down = gate_ref[0], up_ref[0], down_ref[0]
    gate_pre = jnp.dot(codes, gate, preferred_element_type=f32)
    up_pre = jnp.dot(codes, up, preferred_element_type=f32)
    nt = (((1,), (1,)), ((), ()))
    tn = (((0,), (0,)), ((), ()))
    d_hidden = lax.dot_general(d_narrow, down, nt, preferred_element_type=f32)
    sig = 0.5 * jnp.tanh(0.5 * gate_pre) + 0.5
    active = gate_pre * sig
    slope = sig * (1.0 + gate_pre - active)
    hidden = (active * up_pre).astype(bf16)
    d_gate = (d_hidden * up_pre * slope).astype(bf16)
    d_up = (d_hidden * active).astype(bf16)
    narrow = jnp.dot(hidden, down, preferred_element_type=f32)
    d_codes = lax.dot_general(d_gate, gate, nt, preferred_element_type=f32) + lax.dot_general(
        d_up, up, nt, preferred_element_type=f32
    )
    grads_ref[0, 0, 0] = lax.dot_general(codes, d_gate, tn, preferred_element_type=f32).astype(bf16)
    grads_ref[0, 0, 1] = lax.dot_general(codes, d_up, tn, preferred_element_type=f32).astype(bf16)
    grads_ref[0, 0, 2] = lax.dot_general(d_narrow, hidden, tn, preferred_element_type=f32).astype(
        bf16
    )

    @pl.when(f == 0)
    def _():
        narrow_acc[...] = narrow
        codes_acc[...] = d_codes

    @pl.when(f > 0)
    def _():
        narrow_acc[...] += narrow
        codes_acc[...] += d_codes

    @pl.when(f == pl.num_programs(1) - 1)
    def _():
        out_ref[e, :, 0:rank] = narrow_acc[...].astype(bf16)
        out_ref[e, :, rank:] = codes_acc[...].astype(bf16)
        for i, ref in enumerate(outs):
            rows = pl.ds(i * slots, slots)
            pltpu.make_async_copy(out_ref.at[e, rows], ref.at[e], sem.at[e, i]).start()

        @pl.when(e == pl.num_programs(0) - 1)
        def _():
            for at in range(EXP_DEV):
                for i, ref in enumerate(outs):
                    rows = pl.ds(i * slots, slots)
                    pltpu.make_async_copy(out_ref.at[at, rows], ref.at[at], sem.at[at, i]).wait()


def spread_rows(row, route_ref, got, j, slots, tokens, rank):
    hit = one_hot(route_ref, row, slots, tokens)
    pick = jnp.where(hit, 1.0, 0.0).astype(bf16)
    weights = route_ref[pl.ds(len(OWNERS) * EXP_DEV + row, 1), :]
    weight = jnp.sum(jnp.where(hit, weights, 0.0), axis=1, keepdims=True)
    narrow = got[j, :, 0:rank].astype(f32)
    both = jnp.concatenate([(weight * narrow).astype(bf16), got[j, :, rank:]], axis=1)
    tn = (((0,), (0,)), ((), ()))
    spread = lax.dot_general(pick, both, tn, preferred_element_type=f32).astype(bf16)
    return hit, narrow, spread[:, :rank], spread[:, rank:]


def combine_kernel(device_ref, route_ref, sent_ref, *refs):
    (mine_ref, other_ref), refs = refs[:2], refs[2:]
    owners = [ref.at[i] for i in range(NX) for ref in (mine_ref, other_ref)]
    returned, refs = refs[: len(OWNERS)], refs[len(OWNERS) :]
    sums, dz_acc, mixed_acc = refs
    tokens, width = dz_acc.shape
    pair = owners[0].shape[0] // 2
    rank = pair // EXP_DEV
    slots = sent_ref.shape[2]
    n_rows = len(OWNERS) * EXP_DEV
    ids = route_ref[2 * n_rows :, :]
    top = ids.shape[0]
    route_sum = jnp.zeros((top, tokens), f32)
    for first in range(0, len(OWNERS), CORES):
        d_codes, narrows = [], []
        for i in range(first, first + CORES):
            for j in range(EXP_DEV):
                row = i * EXP_DEV + j
                hit, narrow, wide_narrow, wide_codes = spread_rows(
                    row, route_ref, returned[i], j, slots, tokens, rank
                )
                narrows.append(wide_narrow)
                d_codes.append(wide_codes)
                token_weight = route_ref[n_rows + row : n_rows + row + 1, :]
                d_narrow = sent_ref[i, j, :, rank:].astype(f32)
                dots = jnp.sum(narrow * d_narrow, axis=1, keepdims=True)
                by_token = jnp.sum(jnp.where(hit, dots, 0.0), axis=0, keepdims=True)
                by_token = by_token / jnp.where(token_weight > 0.0, token_weight, 1.0)
                route_sum += jnp.where(ids == expert_of(device_ref[0], row).astype(f32), by_token, 0.0)
        p_in = jnp.concatenate([owners[first + i][:pair] for i in range(CORES)], axis=0)
        p_out = jnp.concatenate([owners[first + i][pair:] for i in range(CORES)], axis=0)
        dz = jnp.dot(jnp.concatenate(d_codes, axis=1), p_in, preferred_element_type=f32)
        mixed = jnp.dot(jnp.concatenate(narrows, axis=1), p_out, preferred_element_type=f32)
        dz_acc[...] = dz if first == 0 else dz_acc[...] + dz
        mixed_acc[...] = mixed if first == 0 else mixed_acc[...] + mixed
    tok = tokens // len(BLOCKS)
    for s in range(len(BLOCKS)):
        sums_ref = sums.at[s]
        at = slice(s * tok, (s + 1) * tok)
        sums_ref[:tok] = dz_acc[at].astype(bf16)
        sums_ref[tok : 2 * tok] = mixed_acc[at].astype(bf16)
        route = route_sum[:, at]
        high = route.astype(bf16).astype(f32)
        rest = jnp.zeros((top, width - 2 * tok), f32)
        info = jnp.concatenate([high, route - high, rest], axis=1)
        info = jnp.concatenate([info, jnp.zeros((INFO - top, width), f32)], axis=0)
        sums_ref[2 * tok :] = info.astype(bf16)


def projection_kernel(_, coords_ref, back_ref, route_ref, *refs):
    returned, (keep_ref, give_ref, got_ref) = refs[: len(OWNERS)], refs[len(OWNERS) :]
    d = pl.program_id(0)
    tokens, width = coords_ref.shape
    slots = got_ref.shape[2]
    rank = got_ref.shape[3] // 2
    tn = (((0,), (0,)), ((), ()))
    part = width // NY

    @pl.when(d == 0)
    def _():
        for i, ref in enumerate(returned):
            got_ref[i] = ref[...]

    narrows, d_codes = [], []
    for i in range(CORES):
        for j in range(EXP_DEV):
            owner = d * CORES + i
            _, _, narrow, d_code = spread_rows(
                owner * EXP_DEV + j, route_ref, got_ref.at[owner], j, slots, tokens, rank
            )
            narrows.append(narrow)
            d_codes.append(d_code)
    narrows, d_codes = jnp.concatenate(narrows, axis=1), jnp.concatenate(d_codes, axis=1)
    g_in = lax.dot_general(coords_ref[...], d_codes, tn, preferred_element_type=f32).astype(bf16)
    g_out = lax.dot_general(narrows, back_ref[...], tn, preferred_element_type=f32).astype(bf16)
    for i, ref in enumerate((keep_ref, give_ref)):
        for j in range(EXP_DEV):
            col = (i * EXP_DEV + j) * rank
            for y in range(NY):
                at = slice(y * part, (y + 1) * part)
                ref[0, y, j * part : (j + 1) * part, :] = g_in[at, col : col + rank]
                start = EXP_DEV * part + j * rank
                ref[0, y, start : start + rank, :] = g_out[col : col + rank, at]


def finish_kernel(top, own_ref, left_ref, right_ref, *refs):
    line_ref, route_ref = refs[-2:]
    tok = route_ref.shape[1]
    total = own_ref[0].astype(f32) + left_ref[...].astype(f32) + right_ref[...].astype(f32)
    rounded = total[: 2 * tok].astype(bf16)
    for y in range(NY):
        line_ref[y] = rounded
    route = total[2 * tok :]
    route_ref[...] = route[:top, :tok] + route[:top, tok : 2 * tok]


def basis_kernel(device_ref, columns_ref, own_ref, other_ref, _, kept_ref, sent_ref):
    tn = (((0,), (0,)), ((), ()))
    core = lax.rem(device_ref[0], CORES)
    total = None
    for y in range(NY):
        for side, at in ((own_ref, core), (other_ref, 1 - core)):
            term = lax.dot_general(
                columns_ref[CORES * y + at], side[y], tn, preferred_element_type=f32
            )
            total = term if total is None else total + term
    groups, rows, width = kept_ref.shape
    pair = total.astype(bf16).reshape(groups, CORES, rows, width)
    first, second = pair[:, 0], pair[:, 1]
    kept_ref[...] = jnp.where(core == 0, first, second)
    sent_ref[...] = jnp.where(core == 0, second, first)


def tie_kernel(_, out_ref):
    out_ref[...] = jnp.zeros_like(out_ref)


def order_kernel(device_ref, kept_ref, taken_ref, out_ref):
    core = lax.rem(device_ref[0], CORES)
    out_ref[core] = kept_ref[...]
    out_ref[1 - core] = taken_ref[...]


def total_kernel(device_ref, own_ref, up_ref, down_ref, _, *outs):
    y = place_of(device_ref[0])[0]
    for step, out_ref in enumerate(outs):
        at = lax.rem(y + step, NY)
        total = own_ref[at].astype(f32) + up_ref[at].astype(f32) + down_ref[at].astype(f32)
        out_ref[...] = total.astype(bf16)


def plus(a, b):
    return (a.astype(f32) + b.astype(f32)).astype(bf16)


def z_sum(parts):
    at = {step: parts[i] for i, step in enumerate(BLOCKS)}
    left = from_z(at[4], 1)
    first = left
    left = from_z(plus(left, at[-3]), 1)
    right = from_z(at[3], -1)
    for step in (2, 1):
        left, right = from_z(plus(left, at[-step]), 1), from_z(plus(right, at[step]), -1)
    return left, right, first


def ring_sum(parts, move):
    half = parts[2].shape[0] // 2
    up, down = move(parts[2][:half], -1), move(parts[2][half:], 1)
    up = jnp.concatenate([plus(parts[1][:half], up), parts[1][half:]], axis=0)
    down = jnp.concatenate([parts[3][:half], plus(parts[3][half:], down)], axis=0)
    return [parts[0], move(up, -1), move(down, 1)]


def own_kernel(pin_ref, pout_ref, _, out_ref):
    rank = pin_ref.shape[2]
    for j in range(EXP_DEV):
        out_ref[j * rank : (j + 1) * rank] = pin_ref[j].T
        start = (EXP_DEV + j) * rank
        out_ref[start : start + rank] = pout_ref[j]


def stack_kernel(*refs):
    out_ref = refs[-1]
    for i in range(NX):
        out_ref[i] = refs[i][...]


def gathers(payload, own):
    pairs = [own, from_x(own, 1), from_x(own, 3), from_x(own, 2)]
    right, left = [payload], [payload]
    for _ in range(3):
        right.append(from_z(right[-1], -1))
        left.append(from_z(left[-1], 1))
    last = [from_z(right[-1], -1)]
    mine = call(
        stack_kernel,
        (1,),
        [whole(own.shape)] * NX + [pl.BlockSpec(memory_space=pl.ANY)] * 2,
        whole((NX,) + own.shape),
        jax.ShapeDtypeStruct((NX,) + own.shape, own.dtype),
        [],
        (own.size, 4 * MIB),
    )(*pairs, right[3], left[3])
    return [payload] + right[1:] + left[1:] + last, mine, from_core(mine)


def per_device(
    device, activations, cotangent, basis, route_ids, route_weights,
    proj_in, gate_factor, up_factor, down_factor, proj_out,
):
    tok, depth = activations.shape
    top = route_ids.shape[1]
    width = basis.shape[1]
    rank = proj_in.shape[2]
    hidden = gate_factor.shape[2]
    experts = EXP_DEV * CORES * NX * NZ
    cap = max(2, 3 * tok * top // (2 * experts))
    smem, anywhere = pl.BlockSpec(memory_space=pltpu.SMEM), pl.BlockSpec(memory_space=pl.ANY)
    n_own, n_blk = len(OWNERS), len(BLOCKS)
    slots = n_blk * cap
    tokens = n_blk * tok
    rows_e = n_own * EXP_DEV
    pair = EXP_DEV * rank

    steps = NY * CORES
    payload, columns = call(
        embed_kernel,
        (steps,),
        [
            smem,
            pl.BlockSpec((tok, depth // steps), lambda i: (0, i)),
            pl.BlockSpec((tok, depth // steps), lambda i: (0, i)),
            pl.BlockSpec((depth // steps, width), lambda i: (i, 0)),
            whole((top, tok)),
            whole((top, tok)),
        ],
        [
            whole((2 * tok + INFO, width)),
            pl.BlockSpec((1, 2 * tok, depth // steps), lambda i: (i, 0, 0)),
        ],
        [
            jax.ShapeDtypeStruct((2 * tok + INFO, width), bf16),
            jax.ShapeDtypeStruct((steps, 2 * tok, depth // steps), bf16),
        ],
        [pltpu.VMEM((2 * tok, width), f32)],
        (4 * tok * depth * width, 8 * MIB),
    )(device, activations, cotangent, basis, route_ids.T, route_weights.T)

    own = call(
        own_kernel,
        (1,),
        [whole(proj_in.shape), whole(proj_out.shape), anywhere],
        whole((2 * pair, width)),
        jax.ShapeDtypeStruct((2 * pair, width), bf16),
        [],
        (pair * width, MIB),
    )(proj_in, proj_out, payload)
    blocks, *projections = gathers(payload, own)

    tri = (jnp.arange(tok)[:, None] <= jnp.arange(tok)[None, :]).astype(bf16)
    sent, routes, coords_all, back_all = call(
        functools.partial(dispatch_kernel, cap, top),
        (1,),
        [smem, whole((tok, tok))]
        + [whole((2 * tok + INFO, width))] * n_blk
        + [whole((NX, 2 * pair, width))] * 2,
        [
            whole((n_own, EXP_DEV, slots, 2 * rank)),
            whole((2 * rows_e + top, tokens)),
            pl.BlockSpec(memory_space=pl.ANY),
            pl.BlockSpec(memory_space=pl.ANY),
        ],
        [
            jax.ShapeDtypeStruct((n_own, EXP_DEV, slots, 2 * rank), bf16),
            jax.ShapeDtypeStruct((2 * rows_e + top, tokens), f32),
            jax.ShapeDtypeStruct((tokens, width), bf16),
            jax.ShapeDtypeStruct((tokens, width), bf16),
        ],
        [
            pltpu.VMEM((tokens, width), bf16),
            pltpu.VMEM((tokens, width), bf16),
            pltpu.SemaphoreType.DMA((2,)),
        ],
        (n_own * 4 * tokens * width * pair, 9 * MIB),
    )(device, tri, *blocks, *projections)

    got = [sent[i] if i == 0 else to_owner(sent[i], OWNERS[i]) for i in range(n_own)]
    columns = lax.all_to_all(columns, ("dp", "c"), split_axis=0, concat_axis=0, tiled=True)
    block = hidden // NY

    def relative(e, f, device_ref):
        return (f, e, 0, 0, 0)

    *worked, grads = call(
        expert_kernel,
        (EXP_DEV, NY),
        [whole((EXP_DEV, slots, 2 * rank))] * n_own
        + [
            pl.BlockSpec((1, rank, block), lambda e, f, _: (e, 0, f)),
            pl.BlockSpec((1, rank, block), lambda e, f, _: (e, 0, f)),
            pl.BlockSpec((1, block, rank), lambda e, f, _: (e, f, 0)),
        ],
        [pl.BlockSpec(memory_space=pl.ANY)] * n_own
        + [pl.BlockSpec((1, 1, 3, rank, block), relative)],
        [jax.ShapeDtypeStruct((EXP_DEV, slots, 2 * rank), bf16)] * n_own
        + [jax.ShapeDtypeStruct((NY, EXP_DEV, 3, rank, block), bf16)],
        [
            pltpu.VMEM((n_own * slots, rank), f32),
            pltpu.VMEM((n_own * slots, rank), f32),
            pltpu.VMEM((n_own * slots, 2 * rank), bf16),
            pltpu.VMEM((EXP_DEV, n_own * slots, 2 * rank), bf16),
            pltpu.SemaphoreType.DMA((EXP_DEV, n_own)),
        ],
        (EXP_DEV * n_own * slots * rank * hidden * 18, 6 * MIB),
        1,
    )(device, *got, gate_factor, up_factor, down_factor)
    returned = [
        worked[i] if i == 0 else to_owner(worked[i], OWNERS[i], True) for i in range(n_own)
    ]
    part = width // NY
    sums = call(
        combine_kernel,
        (1,),
        [
            smem,
            whole((2 * rows_e + top, tokens)),
            whole((n_own, EXP_DEV, slots, 2 * rank)),
        ]
        + [whole((NX, 2 * pair, width))] * 2
        + [whole((EXP_DEV, slots, 2 * rank))] * n_own,
        whole((n_blk, 2 * tok + INFO, width)),
        jax.ShapeDtypeStruct((n_blk, 2 * tok + INFO, width), bf16),
        [pltpu.VMEM((tokens, width), f32), pltpu.VMEM((tokens, width), f32)],
        (n_own * 4 * tokens * width * pair, 8 * MIB),
    )(device, routes, sent, *projections, *returned)
    left, right, first = z_sum(sums)
    keep, give = call(
        projection_kernel,
        (NX,),
        [
            pl.BlockSpec(memory_space=pl.ANY),
            whole((tokens, width)),
            whole((tokens, width)),
            whole((2 * rows_e + top, tokens)),
        ]
        + [whole((EXP_DEV, slots, 2 * rank))] * n_own,
        [pl.BlockSpec((1, NY, EXP_DEV * part + pair, rank), lambda d: (d, 0, 0, 0))] * 2,
        [jax.ShapeDtypeStruct((NX, NY, EXP_DEV * part + pair, rank), bf16)] * 2,
        [pltpu.VMEM((n_own, EXP_DEV, slots, 2 * rank), bf16)],
        (n_own * 4 * tokens * width * pair, 8 * MIB),
    )(first, coords_all, back_all, routes, *returned)
    on_chip = (keep.astype(f32) + from_core(give).astype(f32)).astype(bf16)

    lines, route = call(
        functools.partial(finish_kernel, top),
        (1,),
        [
            pl.BlockSpec((1, 2 * tok + INFO, width), lambda i: (0, 0, 0)),
            whole((2 * tok + INFO, width)),
            whole((2 * tok + INFO, width)),
            anywhere,
        ],
        [whole((NY, 2 * tok, width)), whole((top, tok))],
        [
            jax.ShapeDtypeStruct((NY, 2 * tok, width), bf16),
            jax.ShapeDtypeStruct((top, tok), f32),
        ],
        [],
        (4 * tok * width, 2 * MIB),
    )(sums, left, right, columns)
    grad_route = route.T

    at_x = {dx: on_chip[i] for i, dx in enumerate(dx for dx, dc in OWNERS if dc == 0)}
    pieces = ring_sum(at_x, from_x)
    dz = lines[0, :tok]
    grad_input = lax.dot_general(
        dz, basis, (((1,), (1,)), ((), ())), preferred_element_type=f32
    ).astype(bf16)

    rows = depth // (NY * NX * NZ * CORES)
    groups = NX * NZ // CORES
    line = lax.all_to_all(lines, "dp", split_axis=0, concat_axis=0, tiled=True)
    tied = call(
        tie_kernel, (1,), [anywhere], whole((8, 128)), jax.ShapeDtypeStruct((8, 128), f32), [], (1, 4096)
    )(line)
    grads, tied = lax.optimization_barrier((grads, tied))
    grads = lax.psum_scatter(grads, "dp", scatter_dimension=0, tiled=False)
    line_other = from_core(line)
    span = depth // steps
    kept, given = call(
        basis_kernel,
        (1,),
        [
            pl.BlockSpec(memory_space=pltpu.SMEM),
            whole((steps, 2 * tok, span)),
            whole((NY, 2 * tok, width)),
            whole((NY, 2 * tok, width)),
            anywhere,
        ],
        [whole((groups, rows, width))] * 2,
        [jax.ShapeDtypeStruct((groups, rows, width), bf16)] * 2,
        [],
        (4 * tok * depth * width, 5 * MIB),
    )(device, columns, line, line_other, tied)
    taken = from_core(given)
    total = call(
        order_kernel,
        (1,),
        [smem, whole((groups, rows, width)), whole((groups, rows, width))],
        whole((CORES, groups, rows, width)),
        jax.ShapeDtypeStruct((CORES, groups, rows, width), bf16),
        [],
        (groups * rows * width, MIB),
    )(device, kept, taken)
    by_y = call(
        total_kernel,
        (1,),
        [smem] + [whole(pieces[0].shape)] * 3 + [anywhere],
        [whole(pieces[0].shape[1:])] * NY,
        [jax.ShapeDtypeStruct(pieces[0].shape[1:], bf16)] * NY,
        [],
        (3 * 4 * MIB, 2 * MIB),
    )(device, *pieces, total)
    total = lax.all_to_all(
        total.reshape(CORES * groups, rows, width), ("x", "z"), split_axis=0, concat_axis=0, tiled=True
    )
    proj = by_y[0].astype(f32)
    for dy in range(1, NY):
        proj = proj + from_y(by_y[dy], -dy).astype(f32)
    grad_proj_in = proj[: EXP_DEV * part].reshape(EXP_DEV, part, rank)
    grad_proj_out = proj[EXP_DEV * part :].reshape(EXP_DEV, rank, part)
    grads = grads.astype(f32)
    grad_gate, grad_up = grads[:, 0], grads[:, 1]
    grad_down = jnp.transpose(grads[:, 2], (0, 2, 1))
    grad_basis = jnp.sum(total.astype(f32), axis=0)
    return (
        grad_input,
        grad_route,
        grad_basis,
        grad_proj_in,
        grad_gate,
        grad_up,
        grad_down,
        grad_proj_out,
    )


def solution(mesh):
    fine = Mesh(mesh.devices.reshape(NY, NX, NZ, CORES), ALL)
    tokens = P(ALL, None)
    expert = P(EXPERT, None, None)
    body = jax.shard_map(
        per_device,
        mesh=fine,
        in_specs=(P(ALL), tokens, tokens, P(), tokens, tokens) + (expert,) * 5,
        out_specs=(
            tokens,
            tokens,
            tokens,
            P(EXPERT, "dp", None),
            P(EXPERT, None, "dp"),
            P(EXPERT, None, "dp"),
            P(EXPERT, "dp", None),
            P(EXPERT, None, "dp"),
        ),
        check_vma=False,
    )
    return lambda *args: body(jnp.arange(mesh.devices.size, dtype=jnp.int32), *args)
```

```python
import functools

import jax
import jax.numpy as jnp
from jax import lax
from jax.experimental import pallas as pl
from jax.experimental.pallas import tpu as pltpu
from jax.sharding import Mesh
from jax.sharding import PartitionSpec as P

EXP_DEV = 2
CORES = 2
NX = 4
NZ = 8
NY = 4
INFO = 16
EXPERT = ("x", "z", "c")
ALL = ("dp", "x", "z", "c")
BLOCKS = (0, -1, -2, -3, 1, 2, 3, 4)
OWNERS = ((0, 0), (0, 1), (1, 0), (1, 1), (3, 0), (3, 1), (2, 0), (2, 1))
f32 = jnp.float32
bf16 = jnp.bfloat16
MIB = 1024 * 1024


def from_z(value, step):
    return lax.ppermute(value, "z", [((z + step) % NZ, z) for z in range(NZ)])


def from_x(value, step):
    return lax.ppermute(value, "x", [((x + step) % NX, x) for x in range(NX)])


def from_y(value, step):
    return lax.ppermute(value, "dp", [((y + step) % NY, y) for y in range(NY)])


def from_core(value):
    return lax.ppermute(value, "c", [(0, 1), (1, 0)])


def to_owner(value, owner, back=False):
    dx, dc = owner
    pairs = [(x * CORES + c, (x + dx) % NX * CORES + (c ^ dc)) for x in range(NX) for c in range(CORES)]
    if back:
        pairs = [(b, a) for a, b in pairs]
    return lax.ppermute(value, ("x", "c"), pairs)


def exchange_sum(parts, axis):
    got = lax.all_to_all(parts, axis, split_axis=0, concat_axis=0, tiled=True)
    return jnp.sum(got.astype(f32), axis=0)


def call(kernel, grid, in_specs, out_specs, out_shape, scratch, cost, prefetch=0):
    return pl.pallas_call(
        kernel,
        grid_spec=pltpu.PrefetchScalarGridSpec(
            num_scalar_prefetch=prefetch,
            grid=grid,
            in_specs=in_specs,
            out_specs=out_specs,
            scratch_shapes=scratch,
        ),
        out_shape=out_shape,
        cost_estimate=pl.CostEstimate(flops=cost[0], bytes_accessed=cost[1], transcendentals=0),
        compiler_params=pltpu.CompilerParams(
            vmem_limit_bytes=24 * MIB, dimension_semantics=("arbitrary",) * len(grid)
        ),
    )


def place_of(device):
    core, rest = lax.rem(device, CORES), lax.div(device, CORES)
    z, rest = lax.rem(rest, NZ), lax.div(rest, NZ)
    return lax.div(rest, NX), lax.rem(rest, NX), z, core


def expert_of(device, row):
    _, x, z, core = place_of(device)
    dx, dc = OWNERS[row // EXP_DEV]
    core = 1 - core if dc else core
    return ((lax.rem(x + dx, NX) * NZ + z) * CORES + core) * EXP_DEV + row % EXP_DEV


def whole(shape):
    return pl.BlockSpec(shape, lambda *_: (0,) * len(shape))


def one_hot(route_ref, row, slots, tokens):
    place = lax.broadcasted_iota(jnp.int32, (slots, tokens), 0).astype(f32)
    return place == route_ref[pl.ds(row, 1), :]


def embed_kernel(_, act_ref, cot_ref, basis_ref, ids_ref, w_ref, out_ref, parts_ref, acc):
    k = pl.program_id(0)
    tok = act_ref.shape[0]
    top = ids_ref.shape[0]

    @pl.when(k == 0)
    def _():
        acc[...] = jnp.zeros_like(acc)

    both = jnp.concatenate([act_ref[...], cot_ref[...]], axis=0)
    parts_ref[0] = both
    acc[...] += jnp.dot(both, basis_ref[...], preferred_element_type=f32)

    @pl.when(k == pl.num_programs(0) - 1)
    def _():
        out_ref[: 2 * tok] = acc[...].astype(bf16)
        ids = ids_ref[...].astype(f32)
        weights = w_ref[...]
        high = weights.astype(bf16).astype(f32)
        rest = jnp.zeros((top, acc.shape[1] - 3 * tok), f32)
        info = jnp.concatenate([ids, high, weights - high, rest], axis=1)
        info = jnp.concatenate([info, jnp.zeros((INFO - top, acc.shape[1]), f32)], axis=0)
        out_ref[2 * tok :] = info.astype(bf16)


def dispatch_kernel(cap, top, *refs):
    (device_ref, tri_ref), refs = refs[:2], refs[2:]
    blocks, refs = refs[: len(BLOCKS)], refs[len(BLOCKS) :]
    (mine_ref, other_ref), refs = refs[:2], refs[2:]
    owners = [ref.at[i] for i in range(NX) for ref in (mine_ref, other_ref)]
    out_ref, route_ref, coords_out, back_out, coords_ref, back_ref, sem = refs
    tok = tri_ref.shape[0]
    tokens = coords_ref.shape[0]
    slots = len(BLOCKS) * cap
    pair = owners[0].shape[0] // 2
    rank = pair // EXP_DEV
    rows = len(OWNERS) * EXP_DEV
    line = lax.broadcasted_iota(jnp.int32, (rows, 1), 0)
    names = jnp.zeros((rows, 1), f32)
    for row in range(rows):
        names = jnp.where(line == row, expert_of(device_ref[0], row).astype(f32), names)
    for s in range(len(BLOCKS)):
        at = slice(s * tok, (s + 1) * tok)
        coords_ref[at, :] = blocks[s][:tok]
        back_ref[at, :] = blocks[s][tok : 2 * tok]
        info = blocks[s][2 * tok :].astype(f32)
        ids = info[:top, :tok]
        weights = info[:top, tok : 2 * tok] + info[:top, 2 * tok : 3 * tok]
        member = jnp.zeros((rows, tok), f32)
        weighted = jnp.zeros((rows, tok), f32)
        for k in range(top):
            hit = names == ids[k : k + 1, :]
            member = jnp.where(hit, 1.0, member)
            weighted = jnp.where(hit, weights[k : k + 1, :], weighted)
        rank_in = jnp.dot(member.astype(bf16), tri_ref[...], preferred_element_type=f32)
        route_ref[:rows, at] = jnp.where(member > 0.0, rank_in - 1.0 + s * cap, -1.0)
        route_ref[rows : 2 * rows, at] = weighted
        route_ref[2 * rows :, at] = ids
    copies = [
        pltpu.make_async_copy(coords_ref, coords_out, sem.at[0]),
        pltpu.make_async_copy(back_ref, back_out, sem.at[1]),
    ]
    for copy in copies:
        copy.start()
    nt = (((1,), (1,)), ((), ()))
    for i, w_ref in enumerate(owners):
        codes = lax.dot_general(
            coords_ref[...], w_ref[:pair], nt, preferred_element_type=f32
        ).astype(bf16)
        cross = lax.dot_general(
            back_ref[...], w_ref[pair:], nt, preferred_element_type=f32
        ).astype(bf16)
        for j in range(EXP_DEV):
            row = i * EXP_DEV + j
            hit = one_hot(route_ref, row, slots, tokens)
            pick = jnp.where(hit, 1.0, 0.0).astype(bf16)
            weight = jnp.sum(
                jnp.where(hit, route_ref[rows + row : rows + row + 1, :], 0.0),
                axis=1,
                keepdims=True,
            )
            cols = slice(j * rank, (j + 1) * rank)
            both = jnp.concatenate([codes[:, cols], cross[:, cols]], axis=1)
            picked = jnp.dot(pick, both, preferred_element_type=f32)
            out_ref[i, j, :, 0:rank] = picked[:, :rank].astype(bf16)
            out_ref[i, j, :, rank:] = (weight * picked[:, rank:]).astype(bf16)
    for copy in copies:
        copy.wait()


def expert_kernel(_, *refs):
    given_refs, refs = refs[: len(OWNERS)], refs[len(OWNERS) :]
    (gate_ref, up_ref, down_ref), refs = refs[:3], refs[3:]
    outs, refs = refs[: len(OWNERS)], refs[len(OWNERS) :]
    grads_ref, narrow_acc, codes_acc, in_ref, out_ref, sem = refs
    e, f = pl.program_id(0), pl.program_id(1)
    slots = given_refs[0].shape[1]

    @pl.when(f == 0)
    def _():
        for i, ref in enumerate(given_refs):
            in_ref[i * slots : (i + 1) * slots] = ref[e]

    rank = gate_ref.shape[1]
    given = in_ref[...]
    codes, d_narrow = given[:, :rank], given[:, rank:]
    gate, up, down = gate_ref[0], up_ref[0], down_ref[0]
    gate_pre = jnp.dot(codes, gate, preferred_element_type=f32)
    up_pre = jnp.dot(codes, up, preferred_element_type=f32)
    nt = (((1,), (1,)), ((), ()))
    tn = (((0,), (0,)), ((), ()))
    d_hidden = lax.dot_general(d_narrow, down, nt, preferred_element_type=f32)
    sig = 0.5 * jnp.tanh(0.5 * gate_pre) + 0.5
    active = gate_pre * sig
    slope = sig * (1.0 + gate_pre - active)
    hidden = (active * up_pre).astype(bf16)
    d_gate = (d_hidden * up_pre * slope).astype(bf16)
    d_up = (d_hidden * active).astype(bf16)
    narrow = jnp.dot(hidden, down, preferred_element_type=f32)
    d_codes = lax.dot_general(d_gate, gate, nt, preferred_element_type=f32) + lax.dot_general(
        d_up, up, nt, preferred_element_type=f32
    )
    grads_ref[0, 0, 0] = lax.dot_general(codes, d_gate, tn, preferred_element_type=f32).astype(bf16)
    grads_ref[0, 0, 1] = lax.dot_general(codes, d_up, tn, preferred_element_type=f32).astype(bf16)
    grads_ref[0, 0, 2] = lax.dot_general(d_narrow, hidden, tn, preferred_element_type=f32).astype(
        bf16
    )

    @pl.when(f == 0)
    def _():
        narrow_acc[...] = narrow
        codes_acc[...] = d_codes

    @pl.when(f > 0)
    def _():
        narrow_acc[...] += narrow
        codes_acc[...] += d_codes

    @pl.when(f == pl.num_programs(1) - 1)
    def _():
        out_ref[e, :, 0:rank] = narrow_acc[...].astype(bf16)
        out_ref[e, :, rank:] = codes_acc[...].astype(bf16)
        for i, ref in enumerate(outs):
            rows = pl.ds(i * slots, slots)
            pltpu.make_async_copy(out_ref.at[e, rows], ref.at[e], sem.at[e, i]).start()

        @pl.when(e == pl.num_programs(0) - 1)
        def _():
            for at in range(EXP_DEV):
                for i, ref in enumerate(outs):
                    rows = pl.ds(i * slots, slots)
                    pltpu.make_async_copy(out_ref.at[at, rows], ref.at[at], sem.at[at, i]).wait()


def spread_rows(row, route_ref, got, j, slots, tokens, rank):
    hit = one_hot(route_ref, row, slots, tokens)
    pick = jnp.where(hit, 1.0, 0.0).astype(bf16)
    weights = route_ref[pl.ds(len(OWNERS) * EXP_DEV + row, 1), :]
    weight = jnp.sum(jnp.where(hit, weights, 0.0), axis=1, keepdims=True)
    narrow = got[j, :, 0:rank].astype(f32)
    both = jnp.concatenate([(weight * narrow).astype(bf16), got[j, :, rank:]], axis=1)
    tn = (((0,), (0,)), ((), ()))
    spread = lax.dot_general(pick, both, tn, preferred_element_type=f32).astype(bf16)
    return hit, narrow, spread[:, :rank], spread[:, rank:]


def combine_kernel(device_ref, route_ref, sent_ref, *refs):
    (mine_ref, other_ref), refs = refs[:2], refs[2:]
    owners = [ref.at[i] for i in range(NX) for ref in (mine_ref, other_ref)]
    returned, refs = refs[: len(OWNERS)], refs[len(OWNERS) :]
    sums, dz_acc, mixed_acc = refs
    tokens, width = dz_acc.shape
    pair = owners[0].shape[0] // 2
    rank = pair // EXP_DEV
    slots = sent_ref.shape[2]
    n_rows = len(OWNERS) * EXP_DEV
    ids = route_ref[2 * n_rows :, :]
    top = ids.shape[0]
    route_sum = jnp.zeros((top, tokens), f32)
    for first in range(0, len(OWNERS), CORES):
        d_codes, narrows = [], []
        for i in range(first, first + CORES):
            for j in range(EXP_DEV):
                row = i * EXP_DEV + j
                hit, narrow, wide_narrow, wide_codes = spread_rows(
                    row, route_ref, returned[i], j, slots, tokens, rank
                )
                narrows.append(wide_narrow)
                d_codes.append(wide_codes)
                token_weight = route_ref[n_rows + row : n_rows + row + 1, :]
                d_narrow = sent_ref[i, j, :, rank:].astype(f32)
                dots = jnp.sum(narrow * d_narrow, axis=1, keepdims=True)
                by_token = jnp.sum(jnp.where(hit, dots, 0.0), axis=0, keepdims=True)
                by_token = by_token / jnp.where(token_weight > 0.0, token_weight, 1.0)
                route_sum += jnp.where(ids == expert_of(device_ref[0], row).astype(f32), by_token, 0.0)
        p_in = jnp.concatenate([owners[first + i][:pair] for i in range(CORES)], axis=0)
        p_out = jnp.concatenate([owners[first + i][pair:] for i in range(CORES)], axis=0)
        dz = jnp.dot(jnp.concatenate(d_codes, axis=1), p_in, preferred_element_type=f32)
        mixed = jnp.dot(jnp.concatenate(narrows, axis=1), p_out, preferred_element_type=f32)
        dz_acc[...] = dz if first == 0 else dz_acc[...] + dz
        mixed_acc[...] = mixed if first == 0 else mixed_acc[...] + mixed
    tok = tokens // len(BLOCKS)
    for s in range(len(BLOCKS)):
        sums_ref = sums.at[s]
        at = slice(s * tok, (s + 1) * tok)
        sums_ref[:tok] = dz_acc[at].astype(bf16)
        sums_ref[tok : 2 * tok] = mixed_acc[at].astype(bf16)
        route = route_sum[:, at]
        high = route.astype(bf16).astype(f32)
        rest = jnp.zeros((top, width - 2 * tok), f32)
        info = jnp.concatenate([high, route - high, rest], axis=1)
        info = jnp.concatenate([info, jnp.zeros((INFO - top, width), f32)], axis=0)
        sums_ref[2 * tok :] = info.astype(bf16)


def projection_kernel(_, coords_ref, back_ref, route_ref, *refs):
    returned, (keep_ref, give_ref, got_ref) = refs[: len(OWNERS)], refs[len(OWNERS) :]
    d = pl.program_id(0)
    tokens, width = coords_ref.shape
    slots = got_ref.shape[2]
    rank = got_ref.shape[3] // 2
    tn = (((0,), (0,)), ((), ()))
    part = width // NY

    @pl.when(d == 0)
    def _():
        for i, ref in enumerate(returned):
            got_ref[i] = ref[...]

    narrows, d_codes = [], []
    for i in range(CORES):
        for j in range(EXP_DEV):
            owner = d * CORES + i
            _, _, narrow, d_code = spread_rows(
                owner * EXP_DEV + j, route_ref, got_ref.at[owner], j, slots, tokens, rank
            )
            narrows.append(narrow)
            d_codes.append(d_code)
    narrows, d_codes = jnp.concatenate(narrows, axis=1), jnp.concatenate(d_codes, axis=1)
    g_in = lax.dot_general(coords_ref[...], d_codes, tn, preferred_element_type=f32).astype(bf16)
    g_out = lax.dot_general(narrows, back_ref[...], tn, preferred_element_type=f32).astype(bf16)
    for i, ref in enumerate((keep_ref, give_ref)):
        for j in range(EXP_DEV):
            col = (i * EXP_DEV + j) * rank
            for y in range(NY):
                at = slice(y * part, (y + 1) * part)
                ref[0, y, j * part : (j + 1) * part, :] = g_in[at, col : col + rank]
                start = EXP_DEV * part + j * rank
                ref[0, y, start : start + rank, :] = g_out[col : col + rank, at]


def finish_kernel(top, own_ref, left_ref, right_ref, *refs):
    line_ref, route_ref = refs[-2:]
    tok = route_ref.shape[1]
    total = own_ref[0].astype(f32) + left_ref[...].astype(f32) + right_ref[...].astype(f32)
    rounded = total[: 2 * tok].astype(bf16)
    for y in range(NY):
        line_ref[y] = rounded
    route = total[2 * tok :]
    route_ref[...] = route[:top, :tok] + route[:top, tok : 2 * tok]


def basis_kernel(device_ref, columns_ref, own_ref, other_ref, _, kept_ref, sent_ref):
    tn = (((0,), (0,)), ((), ()))
    core = lax.rem(device_ref[0], CORES)
    total = None
    for y in range(NY):
        for side, at in ((own_ref, core), (other_ref, 1 - core)):
            term = lax.dot_general(
                columns_ref[CORES * y + at], side[y], tn, preferred_element_type=f32
            )
            total = term if total is None else total + term
    groups, rows, width = kept_ref.shape
    pair = total.astype(bf16).reshape(groups, CORES, rows, width)
    first, second = pair[:, 0], pair[:, 1]
    kept_ref[...] = jnp.where(core == 0, first, second)
    sent_ref[...] = jnp.where(core == 0, second, first)


def widen_kernel(grads_ref, gate_ref, up_ref, down_ref):
    for e in range(EXP_DEV):
        gate_ref[e] = grads_ref[e, 0].astype(f32)
        up_ref[e] = grads_ref[e, 1].astype(f32)
        down_ref[e] = grads_ref[e, 2].astype(f32).T


def tie_kernel(_, __, ___, out_ref):
    out_ref[...] = jnp.zeros_like(out_ref)


def order_kernel(device_ref, kept_ref, taken_ref, out_ref):
    core = lax.rem(device_ref[0], CORES)
    out_ref[core] = kept_ref[...]
    out_ref[1 - core] = taken_ref[...]


def total_kernel(device_ref, own_ref, up_ref, down_ref, _, *outs):
    y = place_of(device_ref[0])[0]
    for step, out_ref in enumerate(outs):
        at = lax.rem(y + step, NY)
        total = own_ref[at].astype(f32) + up_ref[at].astype(f32) + down_ref[at].astype(f32)
        out_ref[...] = total.astype(bf16)


def plus(a, b):
    return (a.astype(f32) + b.astype(f32)).astype(bf16)


def z_sum(parts):
    at = {step: parts[i] for i, step in enumerate(BLOCKS)}
    left = from_z(plus(from_z(at[4], 1), at[-3]), 1)
    right = from_z(at[3], -1)
    for step in (2, 1):
        left, right = from_z(plus(left, at[-step]), 1), from_z(plus(right, at[step]), -1)
    return left, right


def ring_sum(parts, move):
    half = parts[2].shape[0] // 2
    up, down = first = move(parts[2][:half], -1), move(parts[2][half:], 1)
    up = jnp.concatenate([plus(parts[1][:half], up), parts[1][half:]], axis=0)
    down = jnp.concatenate([parts[3][:half], plus(parts[3][half:], down)], axis=0)
    return [parts[0], move(up, -1), move(down, 1)], first


def own_kernel(pin_ref, pout_ref, _, out_ref):
    rank = pin_ref.shape[2]
    for j in range(EXP_DEV):
        out_ref[j * rank : (j + 1) * rank] = pin_ref[j].T
        start = (EXP_DEV + j) * rank
        out_ref[start : start + rank] = pout_ref[j]


def forward_kernel(up_ref, down_ref, _, __, up_out, down_out):
    half = up_out.shape[0]
    up_out[...] = up_ref[half:]
    down_out[...] = down_ref[:half]


def stack_kernel(own_ref, up_ref, down_ref, first_ref, second_ref, _, __, out_ref):
    half = first_ref.shape[0]
    for i, ref in enumerate((own_ref, up_ref, down_ref)):
        out_ref[i] = ref[...]
    out_ref[NX - 1, :half] = first_ref[...]
    out_ref[NX - 1, half:] = second_ref[...]


def gathers(payload, own):
    up, down = from_x(own, 1), from_x(own, 3)
    right, left = [payload], [payload]
    for _ in range(3):
        right.append(from_z(right[-1], -1))
        left.append(from_z(left[-1], 1))
    last = [from_z(right[-1], -1)]
    anywhere, part = pl.BlockSpec(memory_space=pl.ANY), (own.shape[0] // 2, own.shape[1])
    up_far, down_far = call(
        forward_kernel,
        (1,),
        [whole(own.shape)] * 2 + [anywhere] * 2,
        [whole(part)] * 2,
        [jax.ShapeDtypeStruct(part, own.dtype)] * 2,
        [],
        (own.size, MIB),
    )(up, down, right[2], left[2])
    mine = call(
        stack_kernel,
        (1,),
        [whole(own.shape)] * 3 + [whole(part)] * 2 + [anywhere] * 2,
        whole((NX,) + own.shape),
        jax.ShapeDtypeStruct((NX,) + own.shape, own.dtype),
        [],
        (own.size, 4 * MIB),
    )(own, up, down, from_x(down_far, 3), from_x(up_far, 1), right[3], left[3])
    return [payload] + right[1:] + left[1:] + last, mine, from_core(mine)


def per_device(
    device, activations, cotangent, basis, route_ids, route_weights,
    proj_in, gate_factor, up_factor, down_factor, proj_out,
):
    tok, depth = activations.shape
    top = route_ids.shape[1]
    width = basis.shape[1]
    rank = proj_in.shape[2]
    hidden = gate_factor.shape[2]
    experts = EXP_DEV * CORES * NX * NZ
    cap = max(2, 3 * tok * top // (2 * experts))
    smem, anywhere = pl.BlockSpec(memory_space=pltpu.SMEM), pl.BlockSpec(memory_space=pl.ANY)
    n_own, n_blk = len(OWNERS), len(BLOCKS)
    slots = n_blk * cap
    tokens = n_blk * tok
    rows_e = n_own * EXP_DEV
    pair = EXP_DEV * rank

    steps = NY * CORES
    payload, columns = call(
        embed_kernel,
        (steps,),
        [
            smem,
            pl.BlockSpec((tok, depth // steps), lambda i: (0, i)),
            pl.BlockSpec((tok, depth // steps), lambda i: (0, i)),
            pl.BlockSpec((depth // steps, width), lambda i: (i, 0)),
            whole((top, tok)),
            whole((top, tok)),
        ],
        [
            whole((2 * tok + INFO, width)),
            pl.BlockSpec((1, 2 * tok, depth // steps), lambda i: (i, 0, 0)),
        ],
        [
            jax.ShapeDtypeStruct((2 * tok + INFO, width), bf16),
            jax.ShapeDtypeStruct((steps, 2 * tok, depth // steps), bf16),
        ],
        [pltpu.VMEM((2 * tok, width), f32)],
        (4 * tok * depth * width, 8 * MIB),
    )(device, activations, cotangent, basis, route_ids.T, route_weights.T)

    own = call(
        own_kernel,
        (1,),
        [whole(proj_in.shape), whole(proj_out.shape), anywhere],
        whole((2 * pair, width)),
        jax.ShapeDtypeStruct((2 * pair, width), bf16),
        [],
        (pair * width, MIB),
    )(proj_in, proj_out, payload)
    blocks, *projections = gathers(payload, own)

    tri = (jnp.arange(tok)[:, None] <= jnp.arange(tok)[None, :]).astype(bf16)
    sent, routes, coords_all, back_all = call(
        functools.partial(dispatch_kernel, cap, top),
        (1,),
        [smem, whole((tok, tok))]
        + [whole((2 * tok + INFO, width))] * n_blk
        + [whole((NX, 2 * pair, width))] * 2,
        [
            whole((n_own, EXP_DEV, slots, 2 * rank)),
            whole((2 * rows_e + top, tokens)),
            pl.BlockSpec(memory_space=pl.ANY),
            pl.BlockSpec(memory_space=pl.ANY),
        ],
        [
            jax.ShapeDtypeStruct((n_own, EXP_DEV, slots, 2 * rank), bf16),
            jax.ShapeDtypeStruct((2 * rows_e + top, tokens), f32),
            jax.ShapeDtypeStruct((tokens, width), bf16),
            jax.ShapeDtypeStruct((tokens, width), bf16),
        ],
        [
            pltpu.VMEM((tokens, width), bf16),
            pltpu.VMEM((tokens, width), bf16),
            pltpu.SemaphoreType.DMA((2,)),
        ],
        (n_own * 4 * tokens * width * pair, 9 * MIB),
    )(device, tri, *blocks, *projections)

    got = [sent[i] if i == 0 else to_owner(sent[i], OWNERS[i]) for i in range(n_own)]
    block = hidden // NY

    def relative(e, f, device_ref):
        return (f, e, 0, 0, 0)

    *worked, grads = call(
        expert_kernel,
        (EXP_DEV, NY),
        [whole((EXP_DEV, slots, 2 * rank))] * n_own
        + [
            pl.BlockSpec((1, rank, block), lambda e, f, _: (e, 0, f)),
            pl.BlockSpec((1, rank, block), lambda e, f, _: (e, 0, f)),
            pl.BlockSpec((1, block, rank), lambda e, f, _: (e, f, 0)),
        ],
        [pl.BlockSpec(memory_space=pl.ANY)] * n_own
        + [pl.BlockSpec((1, 1, 3, rank, block), relative)],
        [jax.ShapeDtypeStruct((EXP_DEV, slots, 2 * rank), bf16)] * n_own
        + [jax.ShapeDtypeStruct((NY, EXP_DEV, 3, rank, block), bf16)],
        [
            pltpu.VMEM((n_own * slots, rank), f32),
            pltpu.VMEM((n_own * slots, rank), f32),
            pltpu.VMEM((n_own * slots, 2 * rank), bf16),
            pltpu.VMEM((EXP_DEV, n_own * slots, 2 * rank), bf16),
            pltpu.SemaphoreType.DMA((EXP_DEV, n_own)),
        ],
        (EXP_DEV * n_own * slots * rank * hidden * 18, 6 * MIB),
        1,
    )(device, *got, gate_factor, up_factor, down_factor)
    returned = [
        worked[i] if i == 0 else to_owner(worked[i], OWNERS[i], True) for i in range(n_own)
    ]
    part = width // NY
    sums = call(
        combine_kernel,
        (1,),
        [
            smem,
            whole((2 * rows_e + top, tokens)),
            whole((n_own, EXP_DEV, slots, 2 * rank)),
        ]
        + [whole((NX, 2 * pair, width))] * 2
        + [whole((EXP_DEV, slots, 2 * rank))] * n_own,
        whole((n_blk, 2 * tok + INFO, width)),
        jax.ShapeDtypeStruct((n_blk, 2 * tok + INFO, width), bf16),
        [pltpu.VMEM((tokens, width), f32), pltpu.VMEM((tokens, width), f32)],
        (n_own * 4 * tokens * width * pair, 8 * MIB),
    )(device, routes, sent, *projections, *returned)
    keep, give = call(
        projection_kernel,
        (NX,),
        [
            pl.BlockSpec(memory_space=pl.ANY),
            whole((tokens, width)),
            whole((tokens, width)),
            whole((2 * rows_e + top, tokens)),
        ]
        + [whole((EXP_DEV, slots, 2 * rank))] * n_own,
        [pl.BlockSpec((1, NY, EXP_DEV * part + pair, rank), lambda d: (d, 0, 0, 0))] * 2,
        [jax.ShapeDtypeStruct((NX, NY, EXP_DEV * part + pair, rank), bf16)] * 2,
        [pltpu.VMEM((n_own, EXP_DEV, slots, 2 * rank), bf16)],
        (n_own * 4 * tokens * width * pair, 8 * MIB),
    )(sums, coords_all, back_all, routes, *returned)
    columns, keep = lax.optimization_barrier((columns, keep))
    columns = lax.all_to_all(columns, ("dp", "c"), split_axis=0, concat_axis=0, tiled=True)
    left, right = z_sum(sums)
    on_chip = (keep.astype(f32) + from_core(give).astype(f32)).astype(bf16)

    lines, route = call(
        functools.partial(finish_kernel, top),
        (1,),
        [
            pl.BlockSpec((1, 2 * tok + INFO, width), lambda i: (0, 0, 0)),
            whole((2 * tok + INFO, width)),
            whole((2 * tok + INFO, width)),
            anywhere,
        ],
        [whole((NY, 2 * tok, width)), whole((top, tok))],
        [
            jax.ShapeDtypeStruct((NY, 2 * tok, width), bf16),
            jax.ShapeDtypeStruct((top, tok), f32),
        ],
        [],
        (4 * tok * width, 2 * MIB),
    )(sums, left, right, columns)
    grad_route = route.T

    at_x = {dx: on_chip[i] for i, dx in enumerate(dx for dx, dc in OWNERS if dc == 0)}
    pieces, first = ring_sum(at_x, from_x)
    dz = lines[0, :tok]
    grad_input = lax.dot_general(
        dz, basis, (((1,), (1,)), ((), ())), preferred_element_type=f32
    ).astype(bf16)

    rows = depth // (NY * NX * NZ * CORES)
    groups = NX * NZ // CORES
    line = lax.all_to_all(lines, "dp", split_axis=0, concat_axis=0, tiled=True)
    tied = call(
        tie_kernel,
        (1,),
        [anywhere] * 3,
        whole((8, 128)),
        jax.ShapeDtypeStruct((8, 128), f32),
        [],
        (1, 4096),
    )(line, on_chip, on_chip)
    grads, tied = lax.optimization_barrier((grads, tied))
    grads = lax.psum_scatter(grads, "dp", scatter_dimension=0, tiled=False)
    line_other = from_core(line)
    span = depth // steps
    kept, given = call(
        basis_kernel,
        (1,),
        [
            pl.BlockSpec(memory_space=pltpu.SMEM),
            whole((steps, 2 * tok, span)),
            whole((NY, 2 * tok, width)),
            whole((NY, 2 * tok, width)),
            anywhere,
        ],
        [whole((groups, rows, width))] * 2,
        [jax.ShapeDtypeStruct((groups, rows, width), bf16)] * 2,
        [],
        (4 * tok * depth * width, 5 * MIB),
    )(device, columns, line, line_other, tied)
    taken = from_core(given)
    total = call(
        order_kernel,
        (1,),
        [smem, whole((groups, rows, width)), whole((groups, rows, width))],
        whole((CORES, groups, rows, width)),
        jax.ShapeDtypeStruct((CORES, groups, rows, width), bf16),
        [],
        (groups * rows * width, MIB),
    )(device, kept, taken)
    by_y = call(
        total_kernel,
        (1,),
        [smem] + [whole(pieces[0].shape)] * 3 + [anywhere],
        [whole(pieces[0].shape[1:])] * NY,
        [jax.ShapeDtypeStruct(pieces[0].shape[1:], bf16)] * NY,
        [],
        (3 * 4 * MIB, 2 * MIB),
    )(device, *pieces, total)
    total = lax.all_to_all(
        total.reshape(CORES * groups, rows, width), ("x", "z"), split_axis=0, concat_axis=0, tiled=True
    )
    proj = by_y[0].astype(f32)
    for dy in range(1, NY):
        proj = proj + from_y(by_y[dy], -dy).astype(f32)
    grad_proj_in = proj[: EXP_DEV * part].reshape(EXP_DEV, part, rank)
    grad_proj_out = proj[EXP_DEV * part :].reshape(EXP_DEV, rank, part)
    grad_gate, grad_up, grad_down = call(
        widen_kernel,
        (1,),
        [whole((EXP_DEV, 3, rank, block))],
        [whole((EXP_DEV, rank, block))] * 2 + [whole((EXP_DEV, block, rank))],
        [jax.ShapeDtypeStruct((EXP_DEV, rank, block), f32)] * 2
        + [jax.ShapeDtypeStruct((EXP_DEV, block, rank), f32)],
        [],
        (EXP_DEV * 3 * rank * block, 2 * MIB),
    )(grads)
    grad_basis = jnp.sum(total.astype(f32), axis=0)
    return (
        grad_input,
        grad_route,
        grad_basis,
        grad_proj_in,
        grad_gate,
        grad_up,
        grad_down,
        grad_proj_out,
    )


def solution(mesh):
    fine = Mesh(mesh.devices.reshape(NY, NX, NZ, CORES), ALL)
    tokens = P(ALL, None)
    expert = P(EXPERT, None, None)
    body = jax.shard_map(
        per_device,
        mesh=fine,
        in_specs=(P(ALL), tokens, tokens, P(), tokens, tokens) + (expert,) * 5,
        out_specs=(
            tokens,
            tokens,
            tokens,
            P(EXPERT, "dp", None),
            P(EXPERT, None, "dp"),
            P(EXPERT, None, "dp"),
            P(EXPERT, "dp", None),
            P(EXPERT, None, "dp"),
        ),
        check_vma=False,
    )
    return lambda *args: body(jnp.arange(mesh.devices.size, dtype=jnp.int32), *args)
```

```python
import functools

import jax
import jax.numpy as jnp
from jax import lax
from jax.experimental import pallas as pl
from jax.experimental.pallas import tpu as pltpu
from jax.sharding import Mesh
from jax.sharding import PartitionSpec as P

EXP_DEV = 2
CORES = 2
NX = 4
NZ = 8
NY = 4
HALVES = 2
INFO = 16
EXPERT = ("x", "z", "c")
ALL = ("dp", "x", "z", "c")
BLOCKS = (0, -1, -2, -3, 1, 2, 3, 4)
OWNERS = ((0, 0), (0, 1), (1, 0), (1, 1), (3, 0), (3, 1), (2, 0), (2, 1))
f32 = jnp.float32
bf16 = jnp.bfloat16
MIB = 1024 * 1024


def from_z(value, step):
    return lax.ppermute(value, "z", [((z + step) % NZ, z) for z in range(NZ)])


def from_x(value, step):
    return lax.ppermute(value, "x", [((x + step) % NX, x) for x in range(NX)])


def from_y(value, step):
    return lax.ppermute(value, "dp", [((y + step) % NY, y) for y in range(NY)])


def from_core(value):
    return lax.ppermute(value, "c", [(0, 1), (1, 0)])


def to_owner(value, owner, back=False):
    dx, dc = owner
    pairs = [(x * CORES + c, (x + dx) % NX * CORES + (c ^ dc)) for x in range(NX) for c in range(CORES)]
    if back:
        pairs = [(b, a) for a, b in pairs]
    return lax.ppermute(value, ("x", "c"), pairs)


def exchange_sum(parts, axis):
    got = lax.all_to_all(parts, axis, split_axis=0, concat_axis=0, tiled=True)
    return jnp.sum(got.astype(f32), axis=0)


def call(kernel, grid, in_specs, out_specs, out_shape, scratch, cost, prefetch=0, vmem=24):
    return pl.pallas_call(
        kernel,
        grid_spec=pltpu.PrefetchScalarGridSpec(
            num_scalar_prefetch=prefetch,
            grid=grid,
            in_specs=in_specs,
            out_specs=out_specs,
            scratch_shapes=scratch,
        ),
        out_shape=out_shape,
        cost_estimate=pl.CostEstimate(flops=cost[0], bytes_accessed=cost[1], transcendentals=0),
        compiler_params=pltpu.CompilerParams(
            vmem_limit_bytes=vmem * MIB, dimension_semantics=("arbitrary",) * len(grid)
        ),
    )


def place_of(device):
    core, rest = lax.rem(device, CORES), lax.div(device, CORES)
    z, rest = lax.rem(rest, NZ), lax.div(rest, NZ)
    return lax.div(rest, NX), lax.rem(rest, NX), z, core


def expert_of(device, row):
    _, x, z, core = place_of(device)
    dx, dc = OWNERS[row // EXP_DEV]
    core = 1 - core if dc else core
    return ((lax.rem(x + dx, NX) * NZ + z) * CORES + core) * EXP_DEV + row % EXP_DEV


def whole(shape):
    return pl.BlockSpec(shape, lambda *_: (0,) * len(shape))


def one_hot(route_ref, row, slots, tokens):
    place = lax.broadcasted_iota(jnp.int32, (slots, tokens), 0).astype(f32)
    return place == route_ref[pl.ds(row, 1), :]


def embed_kernel(_, act_ref, cot_ref, basis_ref, ids_ref, w_ref, out_ref, parts_ref, acc):
    k = pl.program_id(0)
    tok = act_ref.shape[0]
    top = ids_ref.shape[0]

    @pl.when(k == 0)
    def _():
        acc[...] = jnp.zeros_like(acc)

    both = jnp.concatenate([act_ref[...], cot_ref[...]], axis=0)
    parts_ref[0] = both
    acc[...] += jnp.dot(both, basis_ref[...], preferred_element_type=f32)

    @pl.when(k == pl.num_programs(0) - 1)
    def _():
        out_ref[: 2 * tok] = acc[...].astype(bf16)
        ids = ids_ref[...].astype(f32)
        weights = w_ref[...]
        high = weights.astype(bf16).astype(f32)
        rest = jnp.zeros((top, acc.shape[1] - 3 * tok), f32)
        info = jnp.concatenate([ids, high, weights - high, rest], axis=1)
        info = jnp.concatenate([info, jnp.zeros((INFO - top, acc.shape[1]), f32)], axis=0)
        out_ref[2 * tok :] = info.astype(bf16)


def dispatch_kernel(cap, top, *refs):
    (device_ref, tri_ref), refs = refs[:2], refs[2:]
    blocks, refs = refs[: len(BLOCKS)], refs[len(BLOCKS) :]
    (mine_ref, other_ref), refs = refs[:2], refs[2:]
    owners = [ref.at[i] for i in range(NX) for ref in (mine_ref, other_ref)]
    out_ref, route_ref, coords_out, back_out, coords_ref, back_ref, sem = refs
    tok = tri_ref.shape[0]
    tokens = coords_ref.shape[0]
    slots = len(BLOCKS) * cap
    pair = owners[0].shape[0] // 2
    rank = pair // EXP_DEV
    rows = len(OWNERS) * EXP_DEV
    line = lax.broadcasted_iota(jnp.int32, (rows, 1), 0)
    names = jnp.zeros((rows, 1), f32)
    for row in range(rows):
        names = jnp.where(line == row, expert_of(device_ref[0], row).astype(f32), names)
    for s in range(len(BLOCKS)):
        at = slice(s * tok, (s + 1) * tok)
        coords_ref[at, :] = blocks[s][:tok]
        back_ref[at, :] = blocks[s][tok : 2 * tok]
        info = blocks[s][2 * tok :].astype(f32)
        ids = info[:top, :tok]
        weights = info[:top, tok : 2 * tok] + info[:top, 2 * tok : 3 * tok]
        member = jnp.zeros((rows, tok), f32)
        weighted = jnp.zeros((rows, tok), f32)
        for k in range(top):
            hit = names == ids[k : k + 1, :]
            member = jnp.where(hit, 1.0, member)
            weighted = jnp.where(hit, weights[k : k + 1, :], weighted)
        rank_in = jnp.dot(member.astype(bf16), tri_ref[...], preferred_element_type=f32)
        route_ref[:rows, at] = jnp.where(member > 0.0, rank_in - 1.0 + s * cap, -1.0)
        route_ref[rows : 2 * rows, at] = weighted
        route_ref[2 * rows :, at] = ids
    copies = [
        pltpu.make_async_copy(coords_ref, coords_out, sem.at[0]),
        pltpu.make_async_copy(back_ref, back_out, sem.at[1]),
    ]
    for copy in copies:
        copy.start()
    nt = (((1,), (1,)), ((), ()))
    for i, w_ref in enumerate(owners):
        codes = lax.dot_general(
            coords_ref[...], w_ref[:pair], nt, preferred_element_type=f32
        ).astype(bf16)
        cross = lax.dot_general(
            back_ref[...], w_ref[pair:], nt, preferred_element_type=f32
        ).astype(bf16)
        for j in range(EXP_DEV):
            row = i * EXP_DEV + j
            hit = one_hot(route_ref, row, slots, tokens)
            pick = jnp.where(hit, 1.0, 0.0).astype(bf16)
            weight = jnp.sum(
                jnp.where(hit, route_ref[rows + row : rows + row + 1, :], 0.0),
                axis=1,
                keepdims=True,
            )
            cols = slice(j * rank, (j + 1) * rank)
            both = jnp.concatenate([codes[:, cols], cross[:, cols]], axis=1)
            picked = jnp.dot(pick, both, preferred_element_type=f32)
            out_ref[i, j, :, 0:rank] = picked[:, :rank].astype(bf16)
            out_ref[i, j, :, rank:] = (weight * picked[:, rank:]).astype(bf16)
    for copy in copies:
        copy.wait()


def expert_kernel(_, *refs):
    given_refs, refs = refs[: len(OWNERS)], refs[len(OWNERS) :]
    (gate_ref, up_ref, down_ref), refs = refs[:3], refs[3:]
    outs, refs = refs[: len(OWNERS)], refs[len(OWNERS) :]
    grads_ref, narrow_acc, codes_acc, in_ref, out_ref, sem = refs
    e, f = pl.program_id(0), pl.program_id(1)
    slots = given_refs[0].shape[1]

    @pl.when(f == 0)
    def _():
        for i, ref in enumerate(given_refs):
            in_ref[i * slots : (i + 1) * slots] = ref[e]

    rank = gate_ref.shape[1]
    given = in_ref[...]
    codes, d_narrow = given[:, :rank], given[:, rank:]
    gate, up, down = gate_ref[0], up_ref[0], down_ref[0]
    gate_pre = jnp.dot(codes, gate, preferred_element_type=f32)
    up_pre = jnp.dot(codes, up, preferred_element_type=f32)
    nt = (((1,), (1,)), ((), ()))
    tn = (((0,), (0,)), ((), ()))
    d_hidden = lax.dot_general(d_narrow, down, nt, preferred_element_type=f32)
    sig = 0.5 * jnp.tanh(0.5 * gate_pre) + 0.5
    active = gate_pre * sig
    slope = sig * (1.0 + gate_pre - active)
    hidden = (active * up_pre).astype(bf16)
    d_gate = (d_hidden * up_pre * slope).astype(bf16)
    d_up = (d_hidden * active).astype(bf16)
    narrow = jnp.dot(hidden, down, preferred_element_type=f32)
    d_codes = lax.dot_general(d_gate, gate, nt, preferred_element_type=f32) + lax.dot_general(
        d_up, up, nt, preferred_element_type=f32
    )
    sums = [
        lax.dot_general(codes, d_gate, tn, preferred_element_type=f32).astype(bf16),
        lax.dot_general(codes, d_up, tn, preferred_element_type=f32).astype(bf16),
        lax.dot_general(d_narrow, hidden, tn, preferred_element_type=f32).astype(bf16),
    ]
    part = grads_ref.shape[4]
    for k in range(grads_ref.shape[0]):
        for i, total in enumerate(sums):
            grads_ref[k, 0, i] = total[:, k * part : (k + 1) * part]

    @pl.when(f == 0)
    def _():
        narrow_acc[...] = narrow
        codes_acc[...] = d_codes

    @pl.when(f > 0)
    def _():
        narrow_acc[...] += narrow
        codes_acc[...] += d_codes

    @pl.when(f == pl.num_programs(1) - 1)
    def _():
        out_ref[e, :, 0:rank] = narrow_acc[...].astype(bf16)
        out_ref[e, :, rank:] = codes_acc[...].astype(bf16)
        for i, ref in enumerate(outs):
            rows = pl.ds(i * slots, slots)
            pltpu.make_async_copy(out_ref.at[e, rows], ref.at[e], sem.at[e, i]).start()

        @pl.when(e == pl.num_programs(0) - 1)
        def _():
            for at in range(EXP_DEV):
                for i, ref in enumerate(outs):
                    rows = pl.ds(i * slots, slots)
                    pltpu.make_async_copy(out_ref.at[at, rows], ref.at[at], sem.at[at, i]).wait()


def spread_rows(row, route_ref, got, j, slots, tokens, rank):
    hit = one_hot(route_ref, row, slots, tokens)
    pick = jnp.where(hit, 1.0, 0.0).astype(bf16)
    weights = route_ref[pl.ds(len(OWNERS) * EXP_DEV + row, 1), :]
    weight = jnp.sum(jnp.where(hit, weights, 0.0), axis=1, keepdims=True)
    narrow = got[j, :, 0:rank].astype(f32)
    both = jnp.concatenate([(weight * narrow).astype(bf16), got[j, :, rank:]], axis=1)
    tn = (((0,), (0,)), ((), ()))
    spread = lax.dot_general(pick, both, tn, preferred_element_type=f32).astype(bf16)
    return hit, narrow, spread[:, :rank], spread[:, rank:]


def combine_kernel(device_ref, route_ref, sent_ref, *refs):
    (mine_ref, other_ref), refs = refs[:2], refs[2:]
    owners = [ref.at[i] for i in range(NX) for ref in (mine_ref, other_ref)]
    returned, refs = refs[: len(OWNERS)], refs[len(OWNERS) :]
    sums, dz_acc, mixed_acc = refs
    tokens, width = dz_acc.shape
    pair = owners[0].shape[0] // 2
    rank = pair // EXP_DEV
    slots = sent_ref.shape[2]
    n_rows = len(OWNERS) * EXP_DEV
    ids = route_ref[2 * n_rows :, :]
    top = ids.shape[0]
    route_sum = jnp.zeros((top, tokens), f32)
    for first in range(0, len(OWNERS), CORES):
        d_codes, narrows = [], []
        for i in range(first, first + CORES):
            for j in range(EXP_DEV):
                row = i * EXP_DEV + j
                hit, narrow, wide_narrow, wide_codes = spread_rows(
                    row, route_ref, returned[i], j, slots, tokens, rank
                )
                narrows.append(wide_narrow)
                d_codes.append(wide_codes)
                token_weight = route_ref[n_rows + row : n_rows + row + 1, :]
                d_narrow = sent_ref[i, j, :, rank:].astype(f32)
                dots = jnp.sum(narrow * d_narrow, axis=1, keepdims=True)
                by_token = jnp.sum(jnp.where(hit, dots, 0.0), axis=0, keepdims=True)
                by_token = by_token / jnp.where(token_weight > 0.0, token_weight, 1.0)
                route_sum += jnp.where(ids == expert_of(device_ref[0], row).astype(f32), by_token, 0.0)
        p_in = jnp.concatenate([owners[first + i][:pair] for i in range(CORES)], axis=0)
        p_out = jnp.concatenate([owners[first + i][pair:] for i in range(CORES)], axis=0)
        dz = jnp.dot(jnp.concatenate(d_codes, axis=1), p_in, preferred_element_type=f32)
        mixed = jnp.dot(jnp.concatenate(narrows, axis=1), p_out, preferred_element_type=f32)
        dz_acc[...] = dz if first == 0 else dz_acc[...] + dz
        mixed_acc[...] = mixed if first == 0 else mixed_acc[...] + mixed
    tok = tokens // len(BLOCKS)
    for s in range(len(BLOCKS)):
        sums_ref = sums.at[s]
        at = slice(s * tok, (s + 1) * tok)
        sums_ref[:tok] = dz_acc[at].astype(bf16)
        sums_ref[tok : 2 * tok] = mixed_acc[at].astype(bf16)
        route = route_sum[:, at]
        high = route.astype(bf16).astype(f32)
        rest = jnp.zeros((top, width - 2 * tok), f32)
        info = jnp.concatenate([high, route - high, rest], axis=1)
        info = jnp.concatenate([info, jnp.zeros((INFO - top, width), f32)], axis=0)
        sums_ref[2 * tok :] = info.astype(bf16)


def projection_kernel(_, coords_ref, back_ref, route_ref, *refs):
    returned, (keep_ref, give_ref, got_ref) = refs[: len(OWNERS)], refs[len(OWNERS) :]
    d = pl.program_id(0)
    tokens, width = coords_ref.shape
    slots = got_ref.shape[2]
    rank = got_ref.shape[3] // 2
    tn = (((0,), (0,)), ((), ()))
    part = width // NY

    @pl.when(d == 0)
    def _():
        for i, ref in enumerate(returned):
            got_ref[i] = ref[...]

    narrows, d_codes = [], []
    for i in range(CORES):
        for j in range(EXP_DEV):
            owner = d * CORES + i
            _, _, narrow, d_code = spread_rows(
                owner * EXP_DEV + j, route_ref, got_ref.at[owner], j, slots, tokens, rank
            )
            narrows.append(narrow)
            d_codes.append(d_code)
    narrows, d_codes = jnp.concatenate(narrows, axis=1), jnp.concatenate(d_codes, axis=1)
    g_in = lax.dot_general(coords_ref[...], d_codes, tn, preferred_element_type=f32).astype(bf16)
    g_out = lax.dot_general(narrows, back_ref[...], tn, preferred_element_type=f32).astype(bf16)
    for i, ref in enumerate((keep_ref, give_ref)):
        for j in range(EXP_DEV):
            col = (i * EXP_DEV + j) * rank
            for y in range(NY):
                at = slice(y * part, (y + 1) * part)
                ref[0, y, j * part : (j + 1) * part, :] = g_in[at, col : col + rank]
                start = EXP_DEV * part + j * rank
                ref[0, y, start : start + rank, :] = g_out[col : col + rank, at]


def finish_kernel(top, own_ref, left_ref, right_ref, *refs):
    line_ref, route_ref = refs[-2:]
    tok = route_ref.shape[1]
    total = own_ref[0].astype(f32) + left_ref[...].astype(f32) + right_ref[...].astype(f32)
    rounded = total[: 2 * tok].astype(bf16)
    for y in range(NY):
        line_ref[y] = rounded
    route = total[2 * tok :]
    route_ref[...] = route[:top, :tok] + route[:top, tok : 2 * tok]


def basis_kernel(device_ref, columns_ref, own_ref, other_ref, _, kept_ref, sent_ref):
    tn = (((0,), (0,)), ((), ()))
    core = lax.rem(device_ref[0], CORES)
    total = None
    for y in range(NY):
        for side, at in ((own_ref, core), (other_ref, 1 - core)):
            term = lax.dot_general(
                columns_ref[CORES * y + at], side[y], tn, preferred_element_type=f32
            )
            total = term if total is None else total + term
    groups, rows, width = kept_ref.shape
    pair = total.astype(bf16).reshape(groups, CORES, rows, width)
    first, second = pair[:, 0], pair[:, 1]
    kept_ref[...] = jnp.where(core == 0, first, second)
    sent_ref[...] = jnp.where(core == 0, second, first)


def widen_kernel(grads_ref, gate_ref, up_ref, down_ref):
    for e in range(EXP_DEV):
        gate_ref[e] = grads_ref[e, 0].astype(f32)
        up_ref[e] = grads_ref[e, 1].astype(f32)
        down_ref[e] = grads_ref[e, 2].astype(f32).T


def tie_kernel(_, __, ___, out_ref):
    out_ref[...] = jnp.zeros_like(out_ref)


def order_kernel(device_ref, kept_ref, taken_ref, out_ref):
    core = lax.rem(device_ref[0], CORES)
    out_ref[core] = kept_ref[...]
    out_ref[1 - core] = taken_ref[...]


def total_kernel(device_ref, own_ref, up_ref, down_ref, _, *outs):
    y = place_of(device_ref[0])[0]
    for step, out_ref in enumerate(outs):
        at = lax.rem(y + step, NY)
        total = own_ref[at].astype(f32) + up_ref[at].astype(f32) + down_ref[at].astype(f32)
        out_ref[...] = total.astype(bf16)


def plus(a, b):
    return (a.astype(f32) + b.astype(f32)).astype(bf16)


def z_sum(parts):
    at = {step: parts[i] for i, step in enumerate(BLOCKS)}
    left = from_z(plus(from_z(at[4], 1), at[-3]), 1)
    right = from_z(at[3], -1)
    for step in (2, 1):
        left, right = from_z(plus(left, at[-step]), 1), from_z(plus(right, at[step]), -1)
    return left, right


def ring_sum(parts, move):
    half = parts[2].shape[0] // 2
    up, down = first = move(parts[2][:half], -1), move(parts[2][half:], 1)
    up = jnp.concatenate([plus(parts[1][:half], up), parts[1][half:]], axis=0)
    down = jnp.concatenate([parts[3][:half], plus(parts[3][half:], down)], axis=0)
    return [parts[0], move(up, -1), move(down, 1)], first


def own_kernel(pin_ref, pout_ref, _, out_ref):
    rank = pin_ref.shape[2]
    for j in range(EXP_DEV):
        out_ref[j * rank : (j + 1) * rank] = pin_ref[j].T
        start = (EXP_DEV + j) * rank
        out_ref[start : start + rank] = pout_ref[j]


def forward_kernel(up_ref, down_ref, _, __, up_out, down_out):
    half = up_out.shape[0]
    up_out[...] = up_ref[half:]
    down_out[...] = down_ref[:half]


def stack_kernel(own_ref, up_ref, down_ref, first_ref, second_ref, _, __, out_ref):
    half = first_ref.shape[0]
    for i, ref in enumerate((own_ref, up_ref, down_ref)):
        out_ref[i] = ref[...]
    out_ref[NX - 1, :half] = first_ref[...]
    out_ref[NX - 1, half:] = second_ref[...]


def gathers(payload, own):
    up, down = from_x(own, 1), from_x(own, 3)
    right, left = [payload], [payload]
    for _ in range(3):
        right.append(from_z(right[-1], -1))
        left.append(from_z(left[-1], 1))
    last = [from_z(right[-1], -1)]
    anywhere, part = pl.BlockSpec(memory_space=pl.ANY), (own.shape[0] // 2, own.shape[1])
    up_far, down_far = call(
        forward_kernel,
        (1,),
        [whole(own.shape)] * 2 + [anywhere] * 2,
        [whole(part)] * 2,
        [jax.ShapeDtypeStruct(part, own.dtype)] * 2,
        [],
        (own.size, MIB),
    )(up, down, right[2], left[2])
    mine = call(
        stack_kernel,
        (1,),
        [whole(own.shape)] * 3 + [whole(part)] * 2 + [anywhere] * 2,
        whole((NX,) + own.shape),
        jax.ShapeDtypeStruct((NX,) + own.shape, own.dtype),
        [],
        (own.size, 4 * MIB),
    )(own, up, down, from_x(down_far, 3), from_x(up_far, 1), right[3], left[3])
    return [payload] + right[1:] + left[1:] + last, mine, from_core(mine)


def per_device(
    device, activations, cotangent, basis, route_ids, route_weights,
    proj_in, gate_factor, up_factor, down_factor, proj_out,
):
    tok, depth = activations.shape
    top = route_ids.shape[1]
    width = basis.shape[1]
    rank = proj_in.shape[2]
    hidden = gate_factor.shape[2]
    experts = EXP_DEV * CORES * NX * NZ
    cap = max(2, 3 * tok * top // (2 * experts))
    smem, anywhere = pl.BlockSpec(memory_space=pltpu.SMEM), pl.BlockSpec(memory_space=pl.ANY)
    n_own, n_blk = len(OWNERS), len(BLOCKS)
    slots = n_blk * cap
    tokens = n_blk * tok
    rows_e = n_own * EXP_DEV
    pair = EXP_DEV * rank

    steps = NY * CORES
    payload, columns = call(
        embed_kernel,
        (steps,),
        [
            smem,
            pl.BlockSpec((tok, depth // steps), lambda i: (0, i)),
            pl.BlockSpec((tok, depth // steps), lambda i: (0, i)),
            pl.BlockSpec((depth // steps, width), lambda i: (i, 0)),
            whole((top, tok)),
            whole((top, tok)),
        ],
        [
            whole((2 * tok + INFO, width)),
            pl.BlockSpec((1, 2 * tok, depth // steps), lambda i: (i, 0, 0)),
        ],
        [
            jax.ShapeDtypeStruct((2 * tok + INFO, width), bf16),
            jax.ShapeDtypeStruct((steps, 2 * tok, depth // steps), bf16),
        ],
        [pltpu.VMEM((2 * tok, width), f32)],
        (4 * tok * depth * width, 8 * MIB),
    )(device, activations, cotangent, basis, route_ids.T, route_weights.T)

    own = call(
        own_kernel,
        (1,),
        [whole(proj_in.shape), whole(proj_out.shape), anywhere],
        whole((2 * pair, width)),
        jax.ShapeDtypeStruct((2 * pair, width), bf16),
        [],
        (pair * width, MIB),
    )(proj_in, proj_out, payload)
    blocks, *projections = gathers(payload, own)

    tri = (jnp.arange(tok)[:, None] <= jnp.arange(tok)[None, :]).astype(bf16)
    sent, routes, coords_all, back_all = call(
        functools.partial(dispatch_kernel, cap, top),
        (1,),
        [smem, whole((tok, tok))]
        + [whole((2 * tok + INFO, width))] * n_blk
        + [whole((NX, 2 * pair, width))] * 2,
        [
            whole((n_own, EXP_DEV, slots, 2 * rank)),
            whole((2 * rows_e + top, tokens)),
            pl.BlockSpec(memory_space=pl.ANY),
            pl.BlockSpec(memory_space=pl.ANY),
        ],
        [
            jax.ShapeDtypeStruct((n_own, EXP_DEV, slots, 2 * rank), bf16),
            jax.ShapeDtypeStruct((2 * rows_e + top, tokens), f32),
            jax.ShapeDtypeStruct((tokens, width), bf16),
            jax.ShapeDtypeStruct((tokens, width), bf16),
        ],
        [
            pltpu.VMEM((tokens, width), bf16),
            pltpu.VMEM((tokens, width), bf16),
            pltpu.SemaphoreType.DMA((2,)),
        ],
        (n_own * 4 * tokens * width * pair, 9 * MIB),
    )(device, tri, *blocks, *projections)

    got = [sent[i] if i == 0 else to_owner(sent[i], OWNERS[i]) for i in range(n_own)]
    block = hidden // NY

    def relative(e, f, device_ref):
        return (f, e, 0, 0, 0)

    *worked, grads = call(
        expert_kernel,
        (EXP_DEV, HALVES),
        [whole((EXP_DEV, slots, 2 * rank))] * n_own
        + [
            pl.BlockSpec((1, rank, hidden // HALVES), lambda e, f, _: (e, 0, f)),
            pl.BlockSpec((1, rank, hidden // HALVES), lambda e, f, _: (e, 0, f)),
            pl.BlockSpec((1, hidden // HALVES, rank), lambda e, f, _: (e, f, 0)),
        ],
        [pl.BlockSpec(memory_space=pl.ANY)] * n_own
        + [pl.BlockSpec((NY // HALVES, 1, 3, rank, block), relative)],
        [jax.ShapeDtypeStruct((EXP_DEV, slots, 2 * rank), bf16)] * n_own
        + [jax.ShapeDtypeStruct((NY, EXP_DEV, 3, rank, block), bf16)],
        [
            pltpu.VMEM((n_own * slots, rank), f32),
            pltpu.VMEM((n_own * slots, rank), f32),
            pltpu.VMEM((n_own * slots, 2 * rank), bf16),
            pltpu.VMEM((EXP_DEV, n_own * slots, 2 * rank), bf16),
            pltpu.SemaphoreType.DMA((EXP_DEV, n_own)),
        ],
        (EXP_DEV * n_own * slots * rank * hidden * 18, 6 * MIB),
        1,
        40,
    )(device, *got, gate_factor, up_factor, down_factor)
    returned = [
        worked[i] if i == 0 else to_owner(worked[i], OWNERS[i], True) for i in range(n_own)
    ]
    part = width // NY
    sums = call(
        combine_kernel,
        (1,),
        [
            smem,
            whole((2 * rows_e + top, tokens)),
            whole((n_own, EXP_DEV, slots, 2 * rank)),
        ]
        + [whole((NX, 2 * pair, width))] * 2
        + [whole((EXP_DEV, slots, 2 * rank))] * n_own,
        whole((n_blk, 2 * tok + INFO, width)),
        jax.ShapeDtypeStruct((n_blk, 2 * tok + INFO, width), bf16),
        [pltpu.VMEM((tokens, width), f32), pltpu.VMEM((tokens, width), f32)],
        (n_own * 4 * tokens * width * pair, 8 * MIB),
    )(device, routes, sent, *projections, *returned)
    keep, give = call(
        projection_kernel,
        (NX,),
        [
            pl.BlockSpec(memory_space=pl.ANY),
            whole((tokens, width)),
            whole((tokens, width)),
            whole((2 * rows_e + top, tokens)),
        ]
        + [whole((EXP_DEV, slots, 2 * rank))] * n_own,
        [pl.BlockSpec((1, NY, EXP_DEV * part + pair, rank), lambda d: (d, 0, 0, 0))] * 2,
        [jax.ShapeDtypeStruct((NX, NY, EXP_DEV * part + pair, rank), bf16)] * 2,
        [pltpu.VMEM((n_own, EXP_DEV, slots, 2 * rank), bf16)],
        (n_own * 4 * tokens * width * pair, 8 * MIB),
    )(sums, coords_all, back_all, routes, *returned)
    columns, keep = lax.optimization_barrier((columns, keep))
    columns = lax.all_to_all(columns, ("dp", "c"), split_axis=0, concat_axis=0, tiled=True)
    left, right = z_sum(sums)
    on_chip = (keep.astype(f32) + from_core(give).astype(f32)).astype(bf16)

    lines, route = call(
        functools.partial(finish_kernel, top),
        (1,),
        [
            pl.BlockSpec((1, 2 * tok + INFO, width), lambda i: (0, 0, 0)),
            whole((2 * tok + INFO, width)),
            whole((2 * tok + INFO, width)),
            anywhere,
        ],
        [whole((NY, 2 * tok, width)), whole((top, tok))],
        [
            jax.ShapeDtypeStruct((NY, 2 * tok, width), bf16),
            jax.ShapeDtypeStruct((top, tok), f32),
        ],
        [],
        (4 * tok * width, 2 * MIB),
    )(sums, left, right, columns)
    grad_route = route.T

    at_x = {dx: on_chip[i] for i, dx in enumerate(dx for dx, dc in OWNERS if dc == 0)}
    pieces, first = ring_sum(at_x, from_x)
    dz = lines[0, :tok]
    grad_input = lax.dot_general(
        dz, basis, (((1,), (1,)), ((), ())), preferred_element_type=f32
    ).astype(bf16)

    rows = depth // (NY * NX * NZ * CORES)
    groups = NX * NZ // CORES
    line = lax.all_to_all(lines, "dp", split_axis=0, concat_axis=0, tiled=True)
    tied = call(
        tie_kernel,
        (1,),
        [anywhere] * 3,
        whole((8, 128)),
        jax.ShapeDtypeStruct((8, 128), f32),
        [],
        (1, 4096),
    )(line, on_chip, on_chip)
    grads, tied = lax.optimization_barrier((grads, tied))
    grads = lax.psum_scatter(grads, "dp", scatter_dimension=0, tiled=False)
    line_other = from_core(line)
    span = depth // steps
    kept, given = call(
        basis_kernel,
        (1,),
        [
            pl.BlockSpec(memory_space=pltpu.SMEM),
            whole((steps, 2 * tok, span)),
            whole((NY, 2 * tok, width)),
            whole((NY, 2 * tok, width)),
            anywhere,
        ],
        [whole((groups, rows, width))] * 2,
        [jax.ShapeDtypeStruct((groups, rows, width), bf16)] * 2,
        [],
        (4 * tok * depth * width, 5 * MIB),
    )(device, columns, line, line_other, tied)
    taken = from_core(given)
    total = call(
        order_kernel,
        (1,),
        [smem, whole((groups, rows, width)), whole((groups, rows, width))],
        whole((CORES, groups, rows, width)),
        jax.ShapeDtypeStruct((CORES, groups, rows, width), bf16),
        [],
        (groups * rows * width, MIB),
    )(device, kept, taken)
    by_y = call(
        total_kernel,
        (1,),
        [smem] + [whole(pieces[0].shape)] * 3 + [anywhere],
        [whole(pieces[0].shape[1:])] * NY,
        [jax.ShapeDtypeStruct(pieces[0].shape[1:], bf16)] * NY,
        [],
        (3 * 4 * MIB, 2 * MIB),
    )(device, *pieces, total)
    total = lax.all_to_all(
        total.reshape(CORES * groups, rows, width), ("x", "z"), split_axis=0, concat_axis=0, tiled=True
    )
    proj = by_y[0].astype(f32)
    for dy in range(1, NY):
        proj = proj + from_y(by_y[dy], -dy).astype(f32)
    grad_proj_in = proj[: EXP_DEV * part].reshape(EXP_DEV, part, rank)
    grad_proj_out = proj[EXP_DEV * part :].reshape(EXP_DEV, rank, part)
    grad_gate, grad_up, grad_down = call(
        widen_kernel,
        (1,),
        [whole((EXP_DEV, 3, rank, block))],
        [whole((EXP_DEV, rank, block))] * 2 + [whole((EXP_DEV, block, rank))],
        [jax.ShapeDtypeStruct((EXP_DEV, rank, block), f32)] * 2
        + [jax.ShapeDtypeStruct((EXP_DEV, block, rank), f32)],
        [],
        (EXP_DEV * 3 * rank * block, 2 * MIB),
    )(grads)
    grad_basis = jnp.sum(total.astype(f32), axis=0)
    return (
        grad_input,
        grad_route,
        grad_basis,
        grad_proj_in,
        grad_gate,
        grad_up,
        grad_down,
        grad_proj_out,
    )


def solution(mesh):
    fine = Mesh(mesh.devices.reshape(NY, NX, NZ, CORES), ALL)
    tokens = P(ALL, None)
    expert = P(EXPERT, None, None)
    body = jax.shard_map(
        per_device,
        mesh=fine,
        in_specs=(P(ALL), tokens, tokens, P(), tokens, tokens) + (expert,) * 5,
        out_specs=(
            tokens,
            tokens,
            tokens,
            P(EXPERT, "dp", None),
            P(EXPERT, None, "dp"),
            P(EXPERT, None, "dp"),
            P(EXPERT, "dp", None),
            P(EXPERT, None, "dp"),
        ),
        check_vma=False,
    )
    return lambda *args: body(jnp.arange(mesh.devices.size, dtype=jnp.int32), *args)
```
